128 devices in a mesh: row: 16 (over x, z_hi, core), col: 8 (over z_lo, y).
Axes of the slice: x: 4, y: 4, z: 4 (z_hi: 2, z_lo: 2; z = z_hi * 2 + z_lo), core: 2. Of those that a mesh axis runs over, the one named last changes fastest.
Arguments:
- inputs: bfloat16 [2048, 8192], P('row', 'col'), may hold values from -6 to 6
- gate_pre: bfloat16 [2048, 26624], P('col', 'row'), may hold values from -6 to 6
- up_pre: bfloat16 [2048, 26624], P('col', 'row'), may hold values from -6 to 6
- grad_out: bfloat16 [2048, 8192], P('row', 'col'), may hold values from -0.3125 to 0.3125
- down_weight: bfloat16 [26624, 8192], P('row', 'col'), may hold values from -0.0625 to 0.0625
Outputs:
- grad_gate_weight: bfloat16 [8192, 26624], P('col', 'row')
- grad_up_weight: bfloat16 [8192, 26624], P('col', 'row')
- grad_down_weight: bfloat16 [26624, 8192], P('row', 'col')
The draws below stay inside these ranges and needn't reach their ends.
All inputs are finite; a program needn't handle non-finite values.
Results may differ from the reference program's by a relative error of at most 0.0049.
Values may be sent and summed in bfloat16 or wider, within the bound.
A program may use at most 192 MiB of HBM per device.

```python
import jax
import jax.numpy as jnp

D = 8192
FF = 26624
TOKENS = 2048


def block_scale(own_key, dims, cuts, low, largest):
    gain = 1.0
    for axis_at, parts in cuts:
        steps = jax.random.uniform(jax.random.fold_in(jax.random.fold_in(own_key, 6), axis_at), (parts,), jnp.float32, low / len(cuts), largest / len(cuts))
        gain = gain * jnp.repeat(jnp.exp(steps), dims[axis_at] // parts).reshape((-1,) + (1,) * (len(dims) - 1 - axis_at))
    return gain


def noise(own_key, shape, scale, most, pieces=(), dtype=jnp.bfloat16):
    level = block_scale(own_key, shape, pieces, -0.22, 0.18) if pieces else 1.0
    array = jax.random.normal(own_key, shape, jnp.float32) * scale * level
    return jnp.minimum(jnp.maximum(array, -most), most).astype(dtype)


def setup_inputs(seed: int = 0) -> dict:
    arg_keys = jax.random.split(jax.random.key(seed), 6)
    return {
        "inputs": noise(arg_keys[0], (TOKENS, D), 1.0, 6.0, ((0, 16), (1, 8))),
        "gate_pre": noise(arg_keys[1], (TOKENS, FF), 1.0, 6.0, ((0, 8), (1, 16))),
        "up_pre": noise(arg_keys[2], (TOKENS, FF), 1.0, 6.0, ((0, 8), (1, 16))),
        "grad_out": noise(arg_keys[3], (TOKENS, D), (TOKENS ** -0.5), 0.3125, ((0, 16), (1, 8))),
        "down_weight": noise(arg_keys[4], (FF, D), D ** -0.5, 0.0625, ((0, 16), (1, 8))),
    }


def swiglu_backward(gate_pre, up_pre, grad_hidden):
    gate_value = gate_pre.astype(jnp.float32)
    up_value = up_pre.astype(jnp.float32)
    sigmoid_value = jax.nn.sigmoid(gate_value)
    silu_value = gate_value * sigmoid_value
    hidden = (silu_value * up_value).astype(jnp.bfloat16)
    grad_up = (grad_hidden * silu_value).astype(jnp.bfloat16)
    grad_gate = (grad_hidden * up_value * sigmoid_value * (1.0 + gate_value * (1.0 - sigmoid_value))).astype(jnp.bfloat16)
    return hidden, grad_gate, grad_up


def reference(inputs, gate_pre, up_pre, grad_out, down_weight):
    grad_hidden = jnp.dot(grad_out, down_weight.T, preferred_element_type=jnp.float32)
    hidden, grad_gate, grad_up = swiglu_backward(gate_pre, up_pre, grad_hidden)
    grad_down_weight = jnp.dot(hidden.T, grad_out, preferred_element_type=jnp.float32).astype(jnp.bfloat16)
    grad_gate_weight = jnp.dot(inputs.T, grad_gate, preferred_element_type=jnp.float32).astype(jnp.bfloat16)
    grad_up_weight = jnp.dot(inputs.T, grad_up, preferred_element_type=jnp.float32).astype(jnp.bfloat16)
    return grad_gate_weight, grad_up_weight, grad_down_weight
```

```python
import functools

import jax
import jax.numpy as jnp
from jax import lax
from jax.experimental import pallas as pl
from jax.experimental.pallas import tpu as pltpu
from jax.sharding import PartitionSpec as P

MESH = pl.DeviceIdType.MESH
BF = jnp.bfloat16
F32 = jnp.float32

FF = 1664
D = 1024
TOK = 2048
B_CHUNKS = (256, 256)
A_CHUNKS = (256, 256, 128)
BW = sum(B_CHUNKS)
NB = 2 * BW
NA = sum(A_CHUNKS)
CHUNKS = B_CHUNKS + A_CHUNKS
W = BW + NA
OFFS = tuple(sum(CHUNKS[:i]) for i in range(len(CHUNKS)))
NK = len(CHUNKS)
assert NB + NA == FF
N_REMOTE = 190
N_LOCAL = 64


def is_b(k):
    return k < len(B_CHUNKS)


def kernel(
    x_hbm, gate_hbm, up_hbm, go_hbm, down_hbm,
    og_hbm, ou_hbm, od_hbm,
    grad, in_t, gate, up, gh, part, far, near, swap_s, swap_r, dn_b, dn_a,
    hid_t, gg, gu, x_in, x_t, st_g, st_u, st_d,
    send_sem, recv_sem, local_sem,
):
    r = lax.axis_index("row")
    c = lax.axis_index("col")
    x, zh, core = r // 4, (r // 2) % 2, r % 2
    zl, y = c // 4, c % 4
    z = zh * 2 + zl

    def dev(x_, y_, z_, core_):
        return (x_ * 4 + (z_ // 2) * 2 + core_, (z_ % 2) * 4 + y_)

    zp, zm, z2 = (dev(x, y, (z + d) % 4, core) for d in (1, 3, 2))
    xp, xm, x2 = (dev((x + d) % 4, y, z, core) for d in (1, 3, 2))
    yp, ym = (dev(x, (y + d) % 4, z, core) for d in (1, 3))
    sib = dev(x, y, z, 1 - core)
    mate = dev(x, y, zh * 2 + 1 - zl, core)
    y_prev, y_next, y_far = (y + 3) % 4, (y + 1) % 4, (y + 2) % 4

    barrier = pltpu.get_barrier_semaphore()
    peers = (zp, zm, z2, xp, xm, x2, yp, ym, sib)
    for peer in peers:
        pl.semaphore_signal(barrier, inc=1, device_id=peer, device_id_type=MESH)

    counts = {"remote": 0, "local": 0}
    started = []
    sent = set()

    def send(src, dst, to):
        i = counts["remote"]
        counts["remote"] += 1
        copy = pltpu.make_async_remote_copy(
            src_ref=src, dst_ref=dst, send_sem=send_sem.at[i], recv_sem=recv_sem.at[i],
            device_id=to, device_id_type=MESH,
        )
        copy.start()
        started.append(copy)
        return copy

    def local(src, dst):
        i = counts["local"]
        counts["local"] += 1
        copy = pltpu.make_async_copy(src, dst, local_sem.at[i])
        copy.start()
        return copy

    def al(v, n):
        return pl.multiple_of(v, n)

    def token_block(x_, zh_):
        return al(((x_ % 2) * 8 + zh_ * 4 + (x_ // 2) * 2 + core) * 128, 128)

    own_tok = token_block(x, zh)

    def rows_of(buf, tok, lanes):
        return buf.at[:, :, pl.ds(tok, 128)] if lanes else buf.at[:, pl.ds(tok, 128)]

    def one_of(buf, tok, lanes):
        return buf.at[zl, :, pl.ds(tok, 128)] if lanes else buf.at[zl, pl.ds(tok, 128)]

    def cols(k):
        return pl.ds(OFFS[k], CHUNKS[k])

    def out_at(k, plane):
        if is_b(k):
            return pl.ds(al(plane * BW + OFFS[k], 128), CHUNKS[k])
        return pl.ds(OFFS[k] + BW, CHUNKS[k])

    in_copy = local(x_hbm, x_in)
    own_grad = local(go_hbm, one_of(grad, own_tok, False))
    streams = {"g": (gate_hbm, gate), "u": (up_hbm, up)}
    own_chunk = {}
    z_chunk = {}
    ya_c, yb_c = {}, {}

    def load_chunk(s, k):
        hbm, buf = streams[s]
        own_chunk[s, k] = local(hbm.at[:, out_at(k, zl)], buf.at[y * 2 + zl, :, cols(k)])

    def z_send_chunk(s, k):
        hbm, buf = streams[s]
        z_chunk[s, k] = send(hbm.at[:, out_at(k, 1 - zl)], buf.at[y * 2 + zl, :, cols(k)], mate)

    for k in range(NK):
        for s in "gu":
            load_chunk(s, k)
    dn_copies = [
        local(down_hbm.at[pl.ds(al(zl * BW, 128), BW)], dn_b.at[zl]),
        local(down_hbm.at[pl.ds(NB, NA)], dn_a),
    ]

    pl.semaphore_wait(barrier, len(peers))

    def gather_a(buf, k):
        sl = buf.at[pl.ds(y * 2, 2), :, cols(k)]
        return send(sl, sl, yp), send(sl, sl, ym)

    def gather_b(buf, k, first):
        first[0].wait_recv()
        lo = buf.at[y_prev * 2, :, cols(k)]
        one = send(lo, lo, yp)
        first[1].wait_recv()
        hi = buf.at[y_next * 2 + 1, :, cols(k)]
        return one, send(hi, hi, ym)

    def ya(s, k):
        own_chunk[s, k].wait()
        z_chunk[s, k].wait_recv()
        ya_c[s, k] = gather_a(streams[s][1], k)

    def yb(s, k):
        yb_c[s, k] = gather_b(streams[s][1], k, ya_c[s, k])

    def yc(s, k):
        for copy in yb_c[s, k]:
            copy.wait_recv()

    def row_z(src, buf, lanes):
        dst = one_of(buf, own_tok, lanes)
        return [send(src, dst, to) for to in (zp, zm, z2)]

    def row_core(buf, x_, lanes):
        return [
            send(rows_of(buf, token_block(x_, q), lanes), rows_of(buf, token_block(x_, q), lanes), sib)
            for q in range(2)
        ]

    def row_x(buf, lanes, z_copies):
        for copy in z_copies:
            copy.wait_recv()
        out = []
        for to in (xp, xm, x2):
            out.append([
                send(rows_of(buf, token_block(x, q), lanes), rows_of(buf, token_block(x, q), lanes), to)
                for q in range(2)
            ])
        return out, row_core(buf, x, lanes)

    def row_forward(buf, lanes, x_copies, core_copies, j):
        for copy in x_copies[j]:
            copy.wait_recv()
        core_copies += row_core(buf, (x + (3, 1, 2)[j]) % 4, lanes)

    def silu_parts(t, k):
        g = gate[t, :, cols(k)].astype(F32)
        u = up[t, :, cols(k)].astype(F32)
        s = jax.nn.sigmoid(g)
        return g, u, s

    def make_hidden(k):
        yc("g", k)
        yc("u", k)

        def body(t, carry):
            g, u, s = silu_parts(t, k)
            h = (g * s * u).astype(BF)
            hid_t[cols(k), pl.ds(al(t * 256, 256), 256)] = h.T
            return carry

        lax.fori_loop(0, 8, body, 0)

    def nt(a, b):
        return lax.dot_general(a, b, (((1,), (1,)), ((), ())), preferred_element_type=F32)

    def make_partial(k):
        n = CHUNKS[k]

        def body(t, carry):
            rows = pl.ds(al(t * 256, 256), 256)
            if is_b(k):
                acc = nt(grad[0, rows], dn_b[0, pl.ds(OFFS[k], n)])
                acc += nt(grad[1, rows], dn_b[1, pl.ds(OFFS[k], n)])
            else:
                acc = nt(grad[zl, rows], dn_a[pl.ds(OFFS[k] - BW, n)])
            part[t, :, cols(k)] = acc.astype(BF)
            return carry

        lax.fori_loop(0, 8, body, 0)

    rs1, rs2, swaps, ha, hb = {}, {}, {}, {}, {}

    def rs_a(k):
        make_partial(k)
        cc = cols(k)
        rs1[k] = (
            send(part.at[y_far * 2, :, cc], far.at[0, :, cc], yp),
            send(part.at[y_far * 2 + 1, :, cc], far.at[1, :, cc], ym),
            send(part.at[y_next * 2 + 1, :, cc], near.at[0, 1, :, cc], yp),
            send(part.at[y_prev * 2, :, cc], near.at[1, 0, :, cc], ym),
        )

    def rs_b(k):
        cc = cols(k)
        rs1[k][0].wait_recv()
        a = part[y_next * 2, :, cc].astype(F32) + far[0, :, cc].astype(F32)
        part[y_next * 2, :, cc] = a.astype(BF)
        one = send(part.at[y_next * 2, :, cc], near.at[0, 0, :, cc], yp)
        rs1[k][1].wait_recv()
        a = part[y_prev * 2 + 1, :, cc].astype(F32) + far[1, :, cc].astype(F32)
        part[y_prev * 2 + 1, :, cc] = a.astype(BF)
        rs2[k] = (one, send(part.at[y_prev * 2 + 1, :, cc], near.at[1, 1, :, cc], ym))

    def rs_c(k):
        cc = cols(k)
        for copy in (rs1[k][2], rs1[k][3], rs2[k][0], rs2[k][1]):
            copy.wait_recv()
        for q in range(2):
            a = part[y * 2 + q, :, cc].astype(F32)
            a += near[0, q, :, cc].astype(F32) + near[1, q, :, cc].astype(F32)
            if is_b(k):
                gh[y * 2 + q, :, cc] = a.astype(BF)
            else:
                swap_s[q, :, pl.ds(OFFS[k] - BW, CHUNKS[k])] = a.astype(BF)
        if is_b(k):
            ha[k] = gather_a(gh, k)
        else:
            sl = pl.ds(OFFS[k] - BW, CHUNKS[k])
            swaps[k] = send(swap_s.at[:, :, sl], swap_r.at[:, :, sl], mate)

    def rs_d(k):
        swaps[k].wait_recv()
        sl = pl.ds(OFFS[k] - BW, CHUNKS[k])
        for q in range(2):
            a = swap_s[q, :, sl].astype(F32) + swap_r[q, :, sl].astype(F32)
            gh[y * 2 + q, :, cols(k)] = a.astype(BF)
        ha[k] = gather_a(gh, k)

    def hg_b(k):
        hb[k] = gather_b(gh, k, ha[k])

    staged = {}

    def halves(k):
        return (zl, 1 - zl) if is_b(k) else (zl,)

    def clear(kind, k):
        for copy, is_remote in staged.pop((kind, k - 2), ()):
            if is_remote:
                copy.wait_send()
                sent.add(id(copy))
            else:
                copy.wait()

    def ship(kind, k, st, out, by_rows):
        n = CHUNKS[k]
        p = k % 2
        res = []
        for i in range(len(halves(k))):
            src = st.at[p, i, pl.ds(0, n), :] if by_rows else st.at[p, i, :, pl.ds(0, n)]
            dst = out.at[out_at(k, zl), :] if by_rows else out.at[:, out_at(k, zl)]
            res.append((local(src, dst), False) if i == 0 else (send(src, dst, mate), True))
        staged[kind, k] = res

    returned = []

    def down_grad(k):
        clear("d", k)
        n = CHUNKS[k]
        p = k % 2

        def body(m, carry):
            w = pl.ds(al(m * 256, 256), 256)
            for i, h in enumerate(halves(k)):
                acc = jnp.dot(hid_t[cols(k), :], grad[h, :, w], preferred_element_type=F32)
                st_d[p, i, pl.ds(0, n), w] = acc.astype(BF)
            return carry

        lax.fori_loop(0, 4, body, 0)
        ship("d", k, st_d, od_hbm, True)
        returned.extend(copy for copy, is_remote in staged["d", k] if is_remote)

    def weight_grads(k):
        for copy in hb[k]:
            copy.wait_recv()
        clear("g", k)
        clear("u", k)
        n = CHUNKS[k]
        p = k % 2

        def elem(t, carry):
            g, u, s = silu_parts(t, k)
            e = gh[t, :, cols(k)].astype(F32)
            rows = pl.ds(al(t * 256, 256), 256)
            gu[rows, pl.ds(0, n)] = (e * (g * s)).astype(BF)
            gg[rows, pl.ds(0, n)] = (e * u * s * (1.0 + g * (1.0 - s))).astype(BF)
            return carry

        lax.fori_loop(0, 8, elem, 0)

        def body(m, carry):
            w = pl.ds(al(m * 256, 256), 256)
            for i, h in enumerate(halves(k)):
                lhs = in_t[h, w, :]
                acc = jnp.dot(lhs, gg[:, pl.ds(0, n)], preferred_element_type=F32)
                st_g[p, i, w, pl.ds(0, n)] = acc.astype(BF)
                acc = jnp.dot(lhs, gu[:, pl.ds(0, n)], preferred_element_type=F32)
                st_u[p, i, w, pl.ds(0, n)] = acc.astype(BF)
            return carry

        lax.fori_loop(0, 4, body, 0)
        for kind, st, out in (("g", st_g, og_hbm), ("u", st_u, ou_hbm)):
            ship(kind, k, st, out, False)
            returned.extend(copy for copy, is_remote in staged[kind, k] if is_remote)

    z_send_chunk("g", 0)
    z_send_chunk("u", 0)
    grad_z = row_z(go_hbm, grad, False)
    z_send_chunk("g", 1)
    z_send_chunk("u", 1)
    in_copy.wait()
    x_t[...] = x_in[...].T
    own_in = local(x_t, one_of(in_t, own_tok, True))
    ya("g", 0)
    ya("u", 0)
    own_grad.wait()
    grad_x, grad_core = row_x(grad, False, grad_z)
    ya("g", 1)
    z_send_chunk("g", 2)
    z_send_chunk("u", 2)
    yb("g", 0)
    ya("u", 1)
    yb("u", 0)
    dn_z = send(down_hbm.at[pl.ds(al((1 - zl) * BW, 128), BW)], dn_b.at[zl], mate)
    ya("g", 2)
    yb("g", 1)
    z_send_chunk("g", 3)
    z_send_chunk("u", 3)
    make_hidden(0)
    ya("u", 2)
    yb("u", 1)
    z_send_chunk("g", 4)
    z_send_chunk("u", 4)
    in_z = row_z(x_t, in_t, True)
    ya("g", 3)
    yb("g", 2)
    row_forward(grad, False, grad_x, grad_core, 0)
    row_forward(grad, False, grad_x, grad_core, 1)
    ya("u", 3)
    yb("u", 2)
    make_hidden(1)
    row_forward(grad, False, grad_x, grad_core, 2)
    own_in.wait()
    in_x, in_core = row_x(in_t, True, in_z)
    for copy in dn_copies:
        copy.wait()
    dn_z.wait_recv()
    for copy in grad_core:
        copy.wait_recv()
    rs_a(0)
    ya("g", 4)
    yb("g", 3)
    rs_a(1)
    ya("u", 4)
    yb("u", 3)
    rs_b(0)
    rs_a(2)
    yb("g", 4)
    rs_b(1)
    yb("u", 4)
    rs_c(0)
    down_grad(0)
    rs_a(3)
    rs_b(2)
    rs_c(1)
    hg_b(0)
    down_grad(1)
    row_forward(in_t, True, in_x, in_core, 0)
    row_forward(in_t, True, in_x, in_core, 1)
    rs_a(4)
    rs_b(3)
    rs_c(2)
    hg_b(1)
    row_forward(in_t, True, in_x, in_core, 2)
    for copy in in_core:
        copy.wait_recv()
    weight_grads(0)
    rs_d(2)
    rs_b(4)
    rs_c(3)
    make_hidden(2)
    weight_grads(1)
    rs_d(3)
    hg_b(2)
    rs_c(4)
    make_hidden(3)
    down_grad(2)
    rs_d(4)
    hg_b(3)
    make_hidden(4)
    down_grad(3)
    weight_grads(2)
    hg_b(4)
    down_grad(4)
    weight_grads(3)
    weight_grads(4)

    for copies in staged.values():
        for copy, is_remote in copies:
            if not is_remote:
                copy.wait()
    for copy in returned:
        copy.wait_recv()
    for copy in started:
        if id(copy) not in sent:
            copy.wait_send()
    assert counts["remote"] <= N_REMOTE and counts["local"] <= N_LOCAL


def on_device(inputs, gate_pre, up_pre, grad_out, down_weight):
    any_spec = pl.BlockSpec(memory_space=pl.ANY)
    return pl.pallas_call(
        kernel,
        name="swiglu_backward",
        out_shape=(
            jax.ShapeDtypeStruct((D, FF), BF),
            jax.ShapeDtypeStruct((D, FF), BF),
            jax.ShapeDtypeStruct((FF, D), BF),
        ),
        in_specs=[any_spec] * 5,
        out_specs=(any_spec,) * 3,
        scratch_shapes=[
            pltpu.VMEM((2, TOK, D), BF),
            pltpu.VMEM((2, D, TOK), BF),
            pltpu.VMEM((8, 256, W), BF),
            pltpu.VMEM((8, 256, W), BF),
            pltpu.VMEM((8, 256, W), BF),
            pltpu.VMEM((8, 256, W), BF),
            pltpu.VMEM((2, 256, W), BF),
            pltpu.VMEM((2, 2, 256, W), BF),
            pltpu.VMEM((2, 256, NA), BF),
            pltpu.VMEM((2, 256, NA), BF),
            pltpu.VMEM((2, BW, D), BF),
            pltpu.VMEM((NA, D), BF),
            pltpu.VMEM((W, TOK), BF),
            pltpu.VMEM((TOK, 256), BF),
            pltpu.VMEM((TOK, 256), BF),
            pltpu.VMEM((128, D), BF),
            pltpu.VMEM((D, 128), BF),
            pltpu.VMEM((2, 2, D, 256), BF),
            pltpu.VMEM((2, 2, D, 256), BF),
            pltpu.VMEM((2, 2, 256, D), BF),
            pltpu.SemaphoreType.DMA((N_REMOTE,)),
            pltpu.SemaphoreType.DMA((N_REMOTE,)),
            pltpu.SemaphoreType.DMA((N_LOCAL,)),
        ],
        compiler_params=pltpu.CompilerParams(
            collective_id=0, has_side_effects=True, vmem_limit_bytes=62 * 2**20
        ),
        cost_estimate=pl.CostEstimate(
            flops=8 * TOK * D * FF, bytes_accessed=40 * 2**20, transcendentals=TOK * FF
        ),
    )(inputs, gate_pre, up_pre, grad_out, down_weight)


def solution(mesh):
    placed = (P("row", "col"), P("col", "row"), P("col", "row"), P("row", "col"), P("row", "col"))
    return jax.shard_map(
        on_device,
        mesh=mesh,
        in_specs=placed,
        out_specs=(P("col", "row"), P("col", "row"), P("row", "col")),
        check_vma=False,
    )
```

```python
import functools

import jax
import jax.numpy as jnp
from jax import lax
from jax.experimental import pallas as pl
from jax.experimental.pallas import tpu as pltpu
from jax.sharding import PartitionSpec as P

MESH = pl.DeviceIdType.MESH
BF = jnp.bfloat16
F32 = jnp.float32

FF = 1664
D = 1024
TOK = 2048
B_CHUNKS = (256, 256)
A_CHUNKS = (256, 256, 128)
BW = sum(B_CHUNKS)
NB = 2 * BW
NA = sum(A_CHUNKS)
CHUNKS = B_CHUNKS + A_CHUNKS
W = BW + NA
OFFS = tuple(sum(CHUNKS[:i]) for i in range(len(CHUNKS)))
NK = len(CHUNKS)
assert NB + NA == FF
N_REMOTE = 190
N_LOCAL = 64


SCHEDULE = (
    "Zu1", "Au0", "Ag0", "Zg1", "gz0", "Au1", "Ag1", "Zg2", "Zu0", "Xg0",
    "Bu1", "Zu2", "Bg1", "iz0", "Qu0", "Au2", "Fg0", "Ag2", "Zg0", "dz0",
    "H1", "Bu2", "Xg1", "Lg0", "Qg0", "Eg0", "dw0", "P4", "P3", "Fg1",
    "Bg0", "R4", "P2", "Lg1", "Xi0", "Bu0", "Eg1", "dw1", "D1", "P0",
    "Zg3", "Zg4", "R3", "H0", "R0", "Zu4", "P1", "S4", "R2", "S0",
    "S3", "Fi0", "S2", "Zu3", "R1", "G0", "Li0", "S1", "Bg2", "D0",
    "T2", "Ag4", "Ei0", "O0", "G1", "G2", "H2", "Au3", "T4", "Ag3",
    "Au4", "O1", "Bg4", "Bu4", "G4", "T3", "O2", "Bg3", "D2", "H4",
    "Bu3", "D4", "O4", "G3", "H3", "D3", "O3",
)


def is_b(k):
    return k < len(B_CHUNKS)


def kernel(
    x_hbm, gate_hbm, up_hbm, go_hbm, down_hbm,
    og_hbm, ou_hbm, od_hbm,
    grad, in_t, gate, up, gh, part, kept, far, near, swap_s, swap_r, dn_b, dn_a,
    hid_t, gg, gu, x_in, x_t, st_g, st_u, st_d,
    send_sem, recv_sem, local_sem,
):
    r = lax.axis_index("row")
    c = lax.axis_index("col")
    x, zh, core = r // 4, (r // 2) % 2, r % 2
    zl, y = c // 4, c % 4
    z = zh * 2 + zl

    def dev(x_, y_, z_, core_):
        return (x_ * 4 + (z_ // 2) * 2 + core_, (z_ % 2) * 4 + y_)

    zp, zm, z2 = (dev(x, y, (z + d) % 4, core) for d in (1, 3, 2))
    xp, xm = (dev((x + d) % 4, y, z, core) for d in (1, 3))
    yp, ym = (dev(x, (y + d) % 4, z, core) for d in (1, 3))
    sib = dev(x, y, z, 1 - core)
    mate = dev(x, y, zh * 2 + 1 - zl, core)
    y_prev, y_next, y_far = (y + 3) % 4, (y + 1) % 4, (y + 2) % 4

    barrier = pltpu.get_barrier_semaphore()
    peers = (zp, zm, z2, xp, xm, yp, ym, sib)
    for peer in peers:
        pl.semaphore_signal(barrier, inc=1, device_id=peer, device_id_type=MESH)

    counts = {"remote": 0, "local": 0}
    started = []
    sent = set()

    def send(src, dst, to):
        i = counts["remote"]
        counts["remote"] += 1
        copy = pltpu.make_async_remote_copy(
            src_ref=src, dst_ref=dst, send_sem=send_sem.at[i], recv_sem=recv_sem.at[i],
            device_id=to, device_id_type=MESH,
        )
        copy.start()
        started.append(copy)
        return copy

    def local(src, dst):
        i = counts["local"]
        counts["local"] += 1
        copy = pltpu.make_async_copy(src, dst, local_sem.at[i])
        copy.start()
        return copy

    def al(v, n):
        return pl.multiple_of(v, n)

    def token_block(x_, zh_):
        return al(((x_ % 2) * 8 + zh_ * 4 + (x_ // 2) * 2 + core) * 128, 128)

    own_tok = token_block(x, zh)

    def rows_of(buf, tok, lanes):
        return buf.at[:, :, pl.ds(tok, 128)] if lanes else buf.at[:, pl.ds(tok, 128)]

    def one_of(buf, tok, lanes):
        return buf.at[zl, :, pl.ds(tok, 128)] if lanes else buf.at[zl, pl.ds(tok, 128)]

    def cols(k):
        return pl.ds(OFFS[k], CHUNKS[k])

    def out_at(k, plane):
        if is_b(k):
            return pl.ds(al(plane * BW + OFFS[k], 128), CHUNKS[k])
        return pl.ds(OFFS[k] + BW, CHUNKS[k])

    in_copy = local(x_hbm, x_in)
    own_grad = local(go_hbm, one_of(grad, own_tok, False))
    streams = {"g": (gate_hbm, gate), "u": (up_hbm, up)}
    own_chunk = {}
    z_chunk = {}
    ya_c, yb_c = {}, {}

    def load_chunk(s, k):
        hbm, buf = streams[s]
        own_chunk[s, k] = local(hbm.at[:, out_at(k, zl)], buf.at[y * 2 + zl, :, cols(k)])

    def z_send_chunk(s, k):
        hbm, buf = streams[s]
        z_chunk[s, k] = send(hbm.at[:, out_at(k, 1 - zl)], buf.at[y * 2 + zl, :, cols(k)], mate)

    for k in range(NK):
        for s in "gu":
            load_chunk(s, k)
    dn_copies = [
        local(down_hbm.at[pl.ds(al(zl * BW, 128), BW)], dn_b.at[zl]),
        local(down_hbm.at[pl.ds(NB, NA)], dn_a),
    ]

    pl.semaphore_wait(barrier, len(peers))

    def gather_a(buf, k):
        sl = buf.at[pl.ds(y * 2, 2), :, cols(k)]
        return send(sl, sl, yp), send(sl, sl, ym)

    def gather_b(buf, k, first):
        first[0].wait_recv()
        lo = buf.at[y_prev * 2, :, cols(k)]
        one = send(lo, lo, yp)
        first[1].wait_recv()
        hi = buf.at[y_next * 2 + 1, :, cols(k)]
        return one, send(hi, hi, ym)

    def ya(s, k):
        hbm, buf = streams[s]
        if k == 0:
            dst = buf.at[y * 2 + zl, :, cols(k)]
            src = hbm.at[:, out_at(k, zl)]
            ya_c[s, k] = send(src, dst, yp), send(src, dst, ym)
            return
        own_chunk[s, k].wait()
        z_chunk[s, k].wait_recv()
        ya_c[s, k] = gather_a(buf, k)

    def yq(s, k):
        buf = streams[s][1]
        own_chunk[s, k].wait()
        z_chunk[s, k].wait_recv()
        other = buf.at[y * 2 + 1 - zl, :, cols(k)]
        ya_c[s, k] += send(other, other, yp), send(other, other, ym)

    def yb(s, k):
        buf = streams[s][1]
        if k == 0:
            own_p, own_m, other_p, other_m = ya_c[s, k]
            own_p.wait_recv()
            lo = buf.at[y_prev * 2 + zl, :, cols(k)]
            one = send(lo, lo, yp)
            other_m.wait_recv()
            hi = buf.at[y_next * 2 + 1 - zl, :, cols(k)]
            yb_c[s, k] = one, send(hi, hi, ym), own_m, other_p
            return
        yb_c[s, k] = gather_b(buf, k, ya_c[s, k])

    def yc(s, k):
        for copy in yb_c[s, k]:
            copy.wait_recv()

    def row_z(src, buf, lanes):
        dst = one_of(buf, own_tok, lanes)
        return [send(src, dst, to) for to in (z2, zp, zm)]

    def block(buf, x_, q, which, lanes):
        tok = pl.ds(token_block((x + x_) % 4, q), 128)
        if which == "both":
            return buf.at[:, :, tok] if lanes else buf.at[:, tok]
        half = zl if which == "own" else 1 - zl
        return buf.at[half, :, tok] if lanes else buf.at[half, tok]

    class Row:
        def __init__(self, buf, which, lanes):
            self.buf, self.which, self.lanes = buf, which, lanes
            self.core = []

        def move(self, x_, q, to):
            ref = block(self.buf, x_, q, self.which, self.lanes)
            return send(ref, ref, to)

        def to_core(self, x_):
            self.core += [self.move(x_, q, sib) for q in range(2)]

        def first(self, waits):
            for wait in waits:
                wait()
            self.up = [self.move(0, q, xp) for q in range(2)]
            self.down = [self.move(0, q, xm) for q in range(2)]
            self.to_core(0)

        def relay(self):
            self.up[0].wait_recv()
            self.far = [self.move(3, 0, xp)]
            self.down[1].wait_recv()
            self.far.append(self.move(1, 1, xm))
            self.up[1].wait_recv()
            self.to_core(3)
            self.down[0].wait_recv()
            self.to_core(1)

        def last(self):
            for copy in self.far:
                copy.wait_recv()
            self.to_core(2)

        def done(self):
            for copy in self.core:
                copy.wait_recv()

    def silu_parts(t, k):
        g = gate[t, :, cols(k)].astype(F32)
        u = up[t, :, cols(k)].astype(F32)
        s = jax.nn.sigmoid(g)
        return g, u, s

    def make_hidden(k):
        yc("g", k)
        yc("u", k)

        def body(t, carry):
            g, u, s = silu_parts(t, k)
            h = (g * s * u).astype(BF)
            hid_t[cols(k), pl.ds(al(t * 256, 256), 256)] = h.T
            return carry

        lax.fori_loop(0, 8, body, 0)

    def nt(a, b):
        return lax.dot_general(a, b, (((1,), (1,)), ((), ())), preferred_element_type=F32)

    def partial_block(k, t):
        n = CHUNKS[k]
        rows = pl.ds(al(t * 256, 256), 256)
        if is_b(k):
            acc = nt(grad[0, rows], dn_b[0, pl.ds(OFFS[k], n)])
            return acc + nt(grad[1, rows], dn_b[1, pl.ds(OFFS[k], n)])
        return nt(grad[zl, rows], dn_a[pl.ds(OFFS[k] - BW, n)])

    def make_sent(k):
        def body(i, carry):
            d = 2 - (i // 2) * (1 - 2 * (i % 2))
            t = ((y + d) % 4) * 2 + (i // 2 + i) % 2
            part[t, :, cols(k)] = partial_block(k, t).astype(BF)
            return carry

        lax.fori_loop(0, 4, body, 0)

    def make_kept(k):
        def body(i, carry):
            d = (i // 2) * (1 + 2 * (i % 2))
            t = ((y + d) % 4) * 2 + i % 2
            kept[i, :, cols(k)] = partial_block(k, t)
            return carry

        lax.fori_loop(0, 4, body, 0)

    rs1, rs2, swaps, ha, hb = {}, {}, {}, {}, {}

    def rs_a(k):
        make_sent(k)
        cc = cols(k)
        rs1[k] = (
            send(part.at[y_far * 2, :, cc], far.at[0, :, cc], yp),
            send(part.at[y_far * 2 + 1, :, cc], far.at[1, :, cc], ym),
            send(part.at[y_next * 2 + 1, :, cc], near.at[0, 1, :, cc], yp),
            send(part.at[y_prev * 2, :, cc], near.at[1, 0, :, cc], ym),
        )
        make_kept(k)

    def rs_b(k):
        cc = cols(k)
        rs1[k][0].wait_recv()
        part[y_next * 2, :, cc] = (kept[2, :, cc] + far[0, :, cc].astype(F32)).astype(BF)
        one = send(part.at[y_next * 2, :, cc], near.at[0, 0, :, cc], yp)
        rs1[k][1].wait_recv()
        part[y_prev * 2 + 1, :, cc] = (kept[3, :, cc] + far[1, :, cc].astype(F32)).astype(BF)
        rs2[k] = (one, send(part.at[y_prev * 2 + 1, :, cc], near.at[1, 1, :, cc], ym))

    def rs_c(k):
        cc = cols(k)
        for copy in (rs1[k][2], rs1[k][3], rs2[k][0], rs2[k][1]):
            copy.wait_recv()
        for q in range(2):
            a = kept[q, :, cc] + near[0, q, :, cc].astype(F32) + near[1, q, :, cc].astype(F32)
            if is_b(k):
                gh[y * 2 + q, :, cc] = a.astype(BF)
            else:
                kept[q, :, cc] = a
                swap_s[q, :, pl.ds(OFFS[k] - BW, CHUNKS[k])] = a.astype(BF)
        if is_b(k):
            ha[k] = gather_a(gh, k)
        else:
            sl = pl.ds(OFFS[k] - BW, CHUNKS[k])
            swaps[k] = send(swap_s.at[:, :, sl], swap_r.at[:, :, sl], mate)

    def rs_d(k):
        swaps[k].wait_recv()
        sl = pl.ds(OFFS[k] - BW, CHUNKS[k])
        for q in range(2):
            a = kept[q, :, cols(k)] + swap_r[q, :, sl].astype(F32)
            gh[y * 2 + q, :, cols(k)] = a.astype(BF)
        ha[k] = gather_a(gh, k)

    def hg_b(k):
        hb[k] = gather_b(gh, k, ha[k])

    staged = {}

    def halves(k):
        return (zl, 1 - zl) if is_b(k) else (zl,)

    def clear(kind, k):
        for copy, is_remote in staged.pop((kind, k - 2), ()):
            if is_remote:
                copy.wait_send()
                sent.add(id(copy))
            else:
                copy.wait()

    def ship(kind, k, st, out, by_rows):
        n = CHUNKS[k]
        p = k % 2
        res = []
        for i in range(len(halves(k))):
            src = st.at[p, i, pl.ds(0, n), :] if by_rows else st.at[p, i, :, pl.ds(0, n)]
            dst = out.at[out_at(k, zl), :] if by_rows else out.at[:, out_at(k, zl)]
            res.append((local(src, dst), False) if i == 0 else (send(src, dst, mate), True))
        staged[kind, k] = res

    returned = []

    def down_grad(k):
        clear("d", k)
        n = CHUNKS[k]
        p = k % 2

        def body(m, carry):
            w = pl.ds(al(m * 256, 256), 256)
            for i, h in enumerate(halves(k)):
                acc = jnp.dot(hid_t[cols(k), :], grad[h, :, w], preferred_element_type=F32)
                st_d[p, i, pl.ds(0, n), w] = acc.astype(BF)
            return carry

        lax.fori_loop(0, 4, body, 0)
        ship("d", k, st_d, od_hbm, True)
        returned.extend(copy for copy, is_remote in staged["d", k] if is_remote)

    def weight_grads(k):
        for copy in hb[k]:
            copy.wait_recv()
        clear("g", k)
        clear("u", k)
        n = CHUNKS[k]
        p = k % 2

        def elem(t, carry):
            g, u, s = silu_parts(t, k)
            e = gh[t, :, cols(k)].astype(F32)
            rows = pl.ds(al(t * 256, 256), 256)
            gu[rows, pl.ds(0, n)] = (e * (g * s)).astype(BF)
            gg[rows, pl.ds(0, n)] = (e * u * s * (1.0 + g * (1.0 - s))).astype(BF)
            return carry

        lax.fori_loop(0, 8, elem, 0)

        def body(m, carry):
            w = pl.ds(al(m * 256, 256), 256)
            for i, h in enumerate(halves(k)):
                lhs = in_t[h, w, :]
                acc = jnp.dot(lhs, gg[:, pl.ds(0, n)], preferred_element_type=F32)
                st_g[p, i, w, pl.ds(0, n)] = acc.astype(BF)
                acc = jnp.dot(lhs, gu[:, pl.ds(0, n)], preferred_element_type=F32)
                st_u[p, i, w, pl.ds(0, n)] = acc.astype(BF)
            return carry

        lax.fori_loop(0, 4, body, 0)
        for kind, st, out in (("g", st_g, og_hbm), ("u", st_u, ou_hbm)):
            ship(kind, k, st, out, False)
            returned.extend(copy for copy, is_remote in staged[kind, k] if is_remote)

    rows = {
        "g0": Row(grad, "own", False),
        "g1": Row(grad, "other", False),
        "i0": Row(in_t, "both", True),
    }
    zs = {}

    def grad_z(k):
        zs["g"] = row_z(go_hbm, grad, False)

    def in_z(k):
        in_copy.wait()
        x_t[...] = x_in[...].T
        zs["own"] = local(x_t, one_of(in_t, own_tok, True))
        zs["i"] = row_z(x_t, in_t, True)

    def row_first(s, k):
        if s == "i":
            waits = [zs["own"].wait] + [copy.wait_recv for copy in zs["i"]]
        elif k == 0:
            waits = [own_grad.wait, zs["g"][0].wait_recv]
        else:
            waits = [copy.wait_recv for copy in zs["g"][1:]]
        rows[s + str(k)].first(waits)

    def down_z(k):
        zs["d"] = send(down_hbm.at[pl.ds(al((1 - zl) * BW, 128), BW)], dn_b.at[zl], mate)

    def down_done(k):
        if k == 0:
            dn_copies[1].wait()
        else:
            dn_copies[0].wait()
            zs["d"].wait_recv()

    events = {
        "Z": z_send_chunk, "A": ya, "Q": yq, "B": yb,
        "X": row_first,
        "F": lambda s, k: rows[s + str(k)].relay(),
        "L": lambda s, k: rows[s + str(k)].last(),
        "E": lambda s, k: rows[s + str(k)].done(),
        "gz": grad_z, "iz": in_z, "dz": down_z, "dw": down_done,
        "H": make_hidden, "P": rs_a, "R": rs_b, "S": rs_c, "T": rs_d, "G": hg_b,
        "D": down_grad, "O": weight_grads,
    }
    for token in SCHEDULE:
        name, k = token[:-1], int(token[-1])
        if name in events:
            events[name](k)
        else:
            events[name[0]](name[1], k)

    for copies in staged.values():
        for copy, is_remote in copies:
            if not is_remote:
                copy.wait()
    for copy in returned:
        copy.wait_recv()
    for copy in started:
        if id(copy) not in sent:
            copy.wait_send()
    assert counts["remote"] <= N_REMOTE and counts["local"] <= N_LOCAL


def on_device(inputs, gate_pre, up_pre, grad_out, down_weight):
    any_spec = pl.BlockSpec(memory_space=pl.ANY)
    return pl.pallas_call(
        kernel,
        name="swiglu_backward",
        out_shape=(
            jax.ShapeDtypeStruct((D, FF), BF),
            jax.ShapeDtypeStruct((D, FF), BF),
            jax.ShapeDtypeStruct((FF, D), BF),
        ),
        in_specs=[any_spec] * 5,
        out_specs=(any_spec,) * 3,
        scratch_shapes=[
            pltpu.VMEM((2, TOK, D), BF),
            pltpu.VMEM((2, D, TOK), BF),
            pltpu.VMEM((8, 256, W), BF),
            pltpu.VMEM((8, 256, W), BF),
            pltpu.VMEM((8, 256, W), BF),
            pltpu.VMEM((8, 256, W), BF),
            pltpu.VMEM((4, 256, W), F32),
            pltpu.VMEM((2, 256, W), BF),
            pltpu.VMEM((2, 2, 256, W), BF),
            pltpu.VMEM((2, 256, NA), BF),
            pltpu.VMEM((2, 256, NA), BF),
            pltpu.VMEM((2, BW, D), BF),
            pltpu.VMEM((NA, D), BF),
            pltpu.VMEM((W, TOK), BF),
            pltpu.VMEM((TOK, 256), BF),
            pltpu.VMEM((TOK, 256), BF),
            pltpu.VMEM((128, D), BF),
            pltpu.VMEM((D, 128), BF),
            pltpu.VMEM((2, 2, D, 256), BF),
            pltpu.VMEM((2, 2, D, 256), BF),
            pltpu.VMEM((2, 2, 256, D), BF),
            pltpu.SemaphoreType.DMA((N_REMOTE,)),
            pltpu.SemaphoreType.DMA((N_REMOTE,)),
            pltpu.SemaphoreType.DMA((N_LOCAL,)),
        ],
        compiler_params=pltpu.CompilerParams(
            collective_id=0, has_side_effects=True, vmem_limit_bytes=62 * 2**20
        ),
        cost_estimate=pl.CostEstimate(
            flops=8 * TOK * D * FF, bytes_accessed=40 * 2**20, transcendentals=TOK * FF
        ),
    )(inputs, gate_pre, up_pre, grad_out, down_weight)


def solution(mesh):
    placed = (P("row", "col"), P("col", "row"), P("col", "row"), P("row", "col"), P("row", "col"))
    return jax.shard_map(
        on_device,
        mesh=mesh,
        in_specs=placed,
        out_specs=(P("col", "row"), P("col", "row"), P("row", "col")),
        check_vma=False,
    )
```

```python
import functools

import jax
import jax.numpy as jnp
from jax import lax
from jax.experimental import pallas as pl
from jax.experimental.pallas import tpu as pltpu
from jax.sharding import PartitionSpec as P

MESH = pl.DeviceIdType.MESH
BF = jnp.bfloat16
F32 = jnp.float32

FF = 1664
D = 1024
TOK = 2048
B_CHUNKS = (256, 256)
S_CHUNKS = (256,)
A_CHUNKS = (256, 128)
BW = sum(B_CHUNKS)
NB = 2 * BW
NS = sum(S_CHUNKS)
NA = NS + sum(A_CHUNKS)
CHUNKS = B_CHUNKS + S_CHUNKS + A_CHUNKS
W = BW + NA
OFFS = tuple(sum(CHUNKS[:i]) for i in range(len(CHUNKS)))
NK = len(CHUNKS)
assert NB + NA == FF
N_REMOTE = 166
N_LOCAL = 40


SCHEDULE = (
    "Zu4", "Au0", "Zu1", "Ag0", "gz0", "Au4", "Au1", "Zg1", "gr0", "Zg0",
    "Xg1", "Bu4", "Zu0", "Ag1", "Zg3", "Qg0", "iz0", "Zg2", "dz0", "Bu1",
    "Ag3", "Qu0", "Bg1", "Xg0", "Fg0", "Bg0", "Bu0", "ir0", "Fg1", "Ag2",
    "Lg0", "Eg0", "dw0", "P3", "H0", "H1", "Lg1", "Xi0", "P4", "R3",
    "Zu2", "R4", "Eg1", "dw1", "P0", "S3", "P1", "Zg4", "Zu3", "D1",
    "R0", "R1", "Fi0", "S0", "D0", "P2", "S4", "G0", "R2", "Li0",
    "S1", "S2", "Au2", "Au3", "Ei0", "O0", "Bg3", "G1", "Bu3", "Bu2",
    "Bg2", "T2", "O1", "Ag4", "H2", "D2", "G2", "H3", "T4", "Bg4",
    "D3", "T3", "O2", "G4", "H4", "G3", "D4", "O4", "O3",
)


def is_b(k):
    return k < len(B_CHUNKS)


def is_s(k):
    return len(B_CHUNKS) <= k < len(B_CHUNKS) + len(S_CHUNKS)


def rs_width(k):
    return CHUNKS[k] // 2 if is_s(k) else CHUNKS[k]


def kernel(
    x_hbm, gate_hbm, up_hbm, go_hbm, down_hbm,
    og_hbm, ou_hbm, od_hbm,
    grad, in_t, gate, up, gh, part, kept, far, near, swap_s, swap_r, dn_b, dn_a,
    hid_t, gg, gu, x_in, x_t, st_g, st_u, st_d,
    send_sem, recv_sem, local_sem,
):
    r = lax.axis_index("row")
    c = lax.axis_index("col")
    x, zh, core = r // 4, (r // 2) % 2, r % 2
    zl, y = c // 4, c % 4
    z = zh * 2 + zl

    def dev(x_, y_, z_, core_):
        return (x_ * 4 + (z_ // 2) * 2 + core_, (z_ % 2) * 4 + y_)

    zo = dev(x, y, (1 - zh) * 2 + 1 - zl, core)
    xp, xm = (dev((x + d) % 4, y, z, core) for d in (1, 3))
    yp, ym = (dev(x, (y + d) % 4, z, core) for d in (1, 3))
    sib = dev(x, y, z, 1 - core)
    mate = dev(x, y, zh * 2 + 1 - zl, core)
    y_prev, y_next, y_far = (y + 3) % 4, (y + 1) % 4, (y + 2) % 4

    barrier = pltpu.get_barrier_semaphore()
    peers = (mate, zo, xp, xm, yp, ym, sib)
    for peer in peers:
        pl.semaphore_signal(barrier, inc=1, device_id=peer, device_id_type=MESH)

    counts = {"remote": 0, "local": 0}
    started = []
    sent = set()

    def send(src, dst, to):
        i = counts["remote"]
        counts["remote"] += 1
        copy = pltpu.make_async_remote_copy(
            src_ref=src, dst_ref=dst, send_sem=send_sem.at[i], recv_sem=recv_sem.at[i],
            device_id=to, device_id_type=MESH,
        )
        copy.start()
        started.append(copy)
        return copy

    def local(src, dst):
        i = counts["local"]
        counts["local"] += 1
        copy = pltpu.make_async_copy(src, dst, local_sem.at[i])
        copy.start()
        return copy

    def al(v, n):
        return pl.multiple_of(v, n)

    def token_block(x_, zh_):
        return al(((x_ % 2) * 8 + zh_ * 4 + (x_ // 2) * 2 + core) * 128, 128)

    own_tok = token_block(x, zh)

    def rows_of(buf, tok, lanes):
        return buf.at[:, :, pl.ds(tok, 128)] if lanes else buf.at[:, pl.ds(tok, 128)]

    def one_of(buf, tok, lanes):
        return buf.at[zl, :, pl.ds(tok, 128)] if lanes else buf.at[zl, pl.ds(tok, 128)]

    def cols(k):
        return pl.ds(OFFS[k], CHUNKS[k])

    def rcols(k):
        return pl.ds(OFFS[k], rs_width(k))

    def dn_at(k):
        return OFFS[k] if is_b(k) else BW + (OFFS[k] - BW) // 2

    def swap_cols(k):
        return pl.ds(OFFS[k] - BW - NS, CHUNKS[k])

    def out_at(k, plane):
        if is_b(k):
            return pl.ds(al(plane * BW + OFFS[k], 128), CHUNKS[k])
        return pl.ds(OFFS[k] + BW, CHUNKS[k])

    def down_parts(plane):
        parts = [(pl.ds(al(plane * BW, 128), BW), pl.ds(0, BW))]
        for k in range(NK):
            if is_s(k):
                n = CHUNKS[k] // 2
                parts.append((
                    pl.ds(al(BW + OFFS[k] + plane * n, 128), n),
                    pl.ds(dn_at(k), n),
                ))
        return parts

    in_copy = local(x_hbm, x_in)
    own_grad = local(go_hbm, one_of(grad, own_tok, False))
    streams = {"g": (gate_hbm, gate), "u": (up_hbm, up)}
    own_chunk = {}
    z_chunk = {}
    ya_c, yb_c = {}, {}

    def load_chunk(s, k):
        hbm, buf = streams[s]
        own_chunk[s, k] = local(hbm.at[:, out_at(k, zl)], buf.at[y * 2 + zl, :, cols(k)])

    def z_send_chunk(s, k):
        hbm, buf = streams[s]
        z_chunk[s, k] = send(hbm.at[:, out_at(k, 1 - zl)], buf.at[y * 2 + zl, :, cols(k)], mate)

    for k in range(NK):
        for s in "gu":
            load_chunk(s, k)
    dn_copies = [
        local(down_hbm.at[src], dn_b.at[zl, dst]) for src, dst in down_parts(zl)
    ]
    dn_copy_a = local(down_hbm.at[pl.ds(NB + NS, NA - NS)], dn_a)

    pl.semaphore_wait(barrier, len(peers))

    def gather_a(buf, k):
        sl = buf.at[pl.ds(y * 2, 2), :, cols(k)]
        return send(sl, sl, yp), send(sl, sl, ym)

    def gather_b(buf, k, first):
        first[0].wait_recv()
        lo = buf.at[y_prev * 2, :, cols(k)]
        one = send(lo, lo, yp)
        first[1].wait_recv()
        hi = buf.at[y_next * 2 + 1, :, cols(k)]
        return one, send(hi, hi, ym)

    def ya(s, k):
        hbm, buf = streams[s]
        if k == 0:
            dst = buf.at[y * 2 + zl, :, cols(k)]
            src = hbm.at[:, out_at(k, zl)]
            ya_c[s, k] = send(src, dst, yp), send(src, dst, ym)
            return
        own_chunk[s, k].wait()
        z_chunk[s, k].wait_recv()
        ya_c[s, k] = gather_a(buf, k)

    def yq(s, k):
        buf = streams[s][1]
        own_chunk[s, k].wait()
        z_chunk[s, k].wait_recv()
        other = buf.at[y * 2 + 1 - zl, :, cols(k)]
        ya_c[s, k] += send(other, other, yp), send(other, other, ym)

    def yb(s, k):
        buf = streams[s][1]
        if k == 0:
            own_p, own_m, other_p, other_m = ya_c[s, k]
            own_p.wait_recv()
            lo = buf.at[y_prev * 2 + zl, :, cols(k)]
            one = send(lo, lo, yp)
            other_m.wait_recv()
            hi = buf.at[y_next * 2 + 1 - zl, :, cols(k)]
            yb_c[s, k] = one, send(hi, hi, ym), own_m, other_p
            return
        yb_c[s, k] = gather_b(buf, k, ya_c[s, k])

    def yc(s, k):
        for copy in yb_c[s, k]:
            copy.wait_recv()

    def row_z(src, buf, lanes):
        dst = one_of(buf, own_tok, lanes)
        return [send(src, dst, to) for to in (mate, zo)]

    def row_z_relay(buf, lanes, copies):
        copies[0].wait_recv()
        tok = pl.ds(own_tok, 128)
        ref = buf.at[1 - zl, :, tok] if lanes else buf.at[1 - zl, tok]
        copies.append(send(ref, ref, zo))

    def block(buf, x_, q, which, lanes):
        tok = pl.ds(token_block((x + x_) % 4, q), 128)
        if which == "both":
            return buf.at[:, :, tok] if lanes else buf.at[:, tok]
        half = zl if which == "own" else 1 - zl
        return buf.at[half, :, tok] if lanes else buf.at[half, tok]

    class Row:
        def __init__(self, buf, which, lanes):
            self.buf, self.which, self.lanes = buf, which, lanes
            self.core = []

        def move(self, x_, q, to):
            ref = block(self.buf, x_, q, self.which, self.lanes)
            return send(ref, ref, to)

        def to_core(self, x_):
            self.core += [self.move(x_, q, sib) for q in range(2)]

        def first(self, waits):
            for wait in waits:
                wait()
            self.up = [self.move(0, q, xp) for q in range(2)]
            self.down = [self.move(0, q, xm) for q in range(2)]
            self.to_core(0)

        def relay(self):
            self.up[0].wait_recv()
            self.far = [self.move(3, 0, xp)]
            self.down[1].wait_recv()
            self.far.append(self.move(1, 1, xm))
            self.up[1].wait_recv()
            self.to_core(3)
            self.down[0].wait_recv()
            self.to_core(1)

        def last(self):
            for copy in self.far:
                copy.wait_recv()
            self.to_core(2)

        def done(self):
            for copy in self.core:
                copy.wait_recv()

    def silu_parts(t, k):
        g = gate[t, :, cols(k)].astype(F32)
        u = up[t, :, cols(k)].astype(F32)
        s = jax.nn.sigmoid(g)
        return g, u, s

    def make_hidden(k):
        yc("g", k)
        yc("u", k)

        def body(t, carry):
            g, u, s = silu_parts(t, k)
            h = (g * s * u).astype(BF)
            hid_t[cols(k), pl.ds(al(t * 256, 256), 256)] = h.T
            return carry

        lax.fori_loop(0, 8, body, 0)

    def nt(a, b):
        return lax.dot_general(a, b, (((1,), (1,)), ((), ())), preferred_element_type=F32)

    def partial_block(k, t):
        n = rs_width(k)
        rows = pl.ds(al(t * 256, 256), 256)
        if is_b(k) or is_s(k):
            acc = nt(grad[0, rows], dn_b[0, pl.ds(dn_at(k), n)])
            return acc + nt(grad[1, rows], dn_b[1, pl.ds(dn_at(k), n)])
        return nt(grad[zl, rows], dn_a[pl.ds(OFFS[k] - BW - NS, n)])

    def make_sent(k):
        def body(i, carry):
            d = 2 - (i // 2) * (1 - 2 * (i % 2))
            t = ((y + d) % 4) * 2 + (i // 2 + i) % 2
            part[t, :, rcols(k)] = partial_block(k, t).astype(BF)
            return carry

        lax.fori_loop(0, 4, body, 0)

    def make_kept(k):
        def body(i, carry):
            d = (i // 2) * (1 + 2 * (i % 2))
            t = ((y + d) % 4) * 2 + i % 2
            kept[i, :, rcols(k)] = partial_block(k, t)
            return carry

        lax.fori_loop(0, 4, body, 0)

    rs1, rs2, swaps, ha, hb = {}, {}, {}, {}, {}

    def rs_a(k):
        make_sent(k)
        cc = rcols(k)
        rs1[k] = (
            send(part.at[y_far * 2, :, cc], far.at[0, :, cc], yp),
            send(part.at[y_far * 2 + 1, :, cc], far.at[1, :, cc], ym),
            send(part.at[y_next * 2 + 1, :, cc], near.at[0, 1, :, cc], yp),
            send(part.at[y_prev * 2, :, cc], near.at[1, 0, :, cc], ym),
        )
        make_kept(k)

    def rs_b(k):
        cc = rcols(k)
        rs1[k][0].wait_recv()
        part[y_next * 2, :, cc] = (kept[2, :, cc] + far[0, :, cc].astype(F32)).astype(BF)
        one = send(part.at[y_next * 2, :, cc], near.at[0, 0, :, cc], yp)
        rs1[k][1].wait_recv()
        part[y_prev * 2 + 1, :, cc] = (kept[3, :, cc] + far[1, :, cc].astype(F32)).astype(BF)
        rs2[k] = (one, send(part.at[y_prev * 2 + 1, :, cc], near.at[1, 1, :, cc], ym))

    def rs_c(k):
        cc = rcols(k)
        n = rs_width(k)
        for copy in (rs1[k][2], rs1[k][3], rs2[k][0], rs2[k][1]):
            copy.wait_recv()
        if is_s(k):
            to = pl.ds(al(OFFS[k] + zl * n, 128), n)
        elif is_b(k):
            to = cols(k)
        for q in range(2):
            a = kept[q, :, cc] + near[0, q, :, cc].astype(F32) + near[1, q, :, cc].astype(F32)
            if is_b(k) or is_s(k):
                gh[y * 2 + q, :, to] = a.astype(BF)
            else:
                kept[q, :, cc] = a
                swap_s[q, :, swap_cols(k)] = a.astype(BF)
        if is_b(k):
            ha[k] = gather_a(gh, k)
        elif is_s(k):
            ref = gh.at[pl.ds(y * 2, 2), :, to]
            swaps[k] = send(ref, ref, mate)
        else:
            swaps[k] = send(swap_s.at[:, :, swap_cols(k)], swap_r.at[:, :, swap_cols(k)], mate)

    def rs_d(k):
        swaps[k].wait_recv()
        if not is_s(k):
            for q in range(2):
                a = kept[q, :, cols(k)] + swap_r[q, :, swap_cols(k)].astype(F32)
                gh[y * 2 + q, :, cols(k)] = a.astype(BF)
        ha[k] = gather_a(gh, k)

    def hg_b(k):
        hb[k] = gather_b(gh, k, ha[k])

    staged = {}

    def halves(k):
        return (zl, 1 - zl) if is_b(k) else (zl,)

    def clear(kind, k):
        for copy, is_remote in staged.pop((kind, k - 2), ()):
            if is_remote:
                copy.wait_send()
                sent.add(id(copy))
            else:
                copy.wait()

    def ship(kind, k, st, out, by_rows):
        n = CHUNKS[k]
        p = k % 2
        res = []
        for i in range(len(halves(k))):
            src = st.at[p, i, pl.ds(0, n), :] if by_rows else st.at[p, i, :, pl.ds(0, n)]
            dst = out.at[out_at(k, zl), :] if by_rows else out.at[:, out_at(k, zl)]
            res.append((local(src, dst), False) if i == 0 else (send(src, dst, mate), True))
        staged[kind, k] = res

    returned = []

    def down_grad(k):
        clear("d", k)
        n = CHUNKS[k]
        p = k % 2

        def body(m, carry):
            w = pl.ds(al(m * 512, 512), 512)
            for i, h in enumerate(halves(k)):
                acc = jnp.dot(hid_t[cols(k), :], grad[h, :, w], preferred_element_type=F32)
                st_d[p, i, pl.ds(0, n), w] = acc.astype(BF)
            return carry

        lax.fori_loop(0, 2, body, 0)
        ship("d", k, st_d, od_hbm, True)
        returned.extend(copy for copy, is_remote in staged["d", k] if is_remote)

    def weight_grads(k):
        for copy in hb[k]:
            copy.wait_recv()
        clear("g", k)
        clear("u", k)
        n = CHUNKS[k]
        p = k % 2

        def elem(t, carry):
            g, u, s = silu_parts(t, k)
            e = gh[t, :, cols(k)].astype(F32)
            rows = pl.ds(al(t * 256, 256), 256)
            gu[rows, pl.ds(0, n)] = (e * (g * s)).astype(BF)
            gg[rows, pl.ds(0, n)] = (e * u * s * (1.0 + g * (1.0 - s))).astype(BF)
            return carry

        lax.fori_loop(0, 8, elem, 0)

        def body(m, carry):
            w = pl.ds(al(m * 1024, 1024), 1024)
            for i, h in enumerate(halves(k)):
                lhs = in_t[h, w, :]
                acc = jnp.dot(lhs, gg[:, pl.ds(0, n)], preferred_element_type=F32)
                st_g[p, i, w, pl.ds(0, n)] = acc.astype(BF)
                acc = jnp.dot(lhs, gu[:, pl.ds(0, n)], preferred_element_type=F32)
                st_u[p, i, w, pl.ds(0, n)] = acc.astype(BF)
            return carry

        lax.fori_loop(0, 1, body, 0)
        for kind, st, out in (("g", st_g, og_hbm), ("u", st_u, ou_hbm)):
            ship(kind, k, st, out, False)
            returned.extend(copy for copy, is_remote in staged[kind, k] if is_remote)

    rows = {
        "g0": Row(grad, "own", False),
        "g1": Row(grad, "other", False),
        "i0": Row(in_t, "both", True),
    }
    zs = {}

    def grad_z(k):
        zs["g"] = row_z(go_hbm, grad, False)

    def in_z(k):
        in_copy.wait()
        x_t[...] = x_in[...].T
        zs["own"] = local(x_t, one_of(in_t, own_tok, True))
        zs["i"] = row_z(x_t, in_t, True)

    def row_first(s, k):
        if s == "i":
            waits = [zs["own"].wait] + [copy.wait_recv for copy in zs["i"][1:]]
        elif k == 0:
            waits = [own_grad.wait, zs["g"][2].wait_recv]
        else:
            waits = [zs["g"][1].wait_recv]
        rows[s + str(k)].first(waits)

    def down_z(k):
        zs["d"] = [send(down_hbm.at[src], dn_b.at[zl, dst], mate) for src, dst in down_parts(1 - zl)]

    def down_done(k):
        if k == 0:
            dn_copy_a.wait()
        else:
            for copy in dn_copies:
                copy.wait()
            for copy in zs["d"]:
                copy.wait_recv()

    events = {
        "Z": z_send_chunk, "A": ya, "Q": yq, "B": yb,
        "X": row_first,
        "F": lambda s, k: rows[s + str(k)].relay(),
        "L": lambda s, k: rows[s + str(k)].last(),
        "E": lambda s, k: rows[s + str(k)].done(),
        "gr": lambda k: row_z_relay(grad, False, zs["g"]),
        "ir": lambda k: row_z_relay(in_t, True, zs["i"]),
        "gz": grad_z, "iz": in_z, "dz": down_z, "dw": down_done,
        "H": make_hidden, "P": rs_a, "R": rs_b, "S": rs_c, "T": rs_d, "G": hg_b,
        "D": down_grad, "O": weight_grads,
    }
    for token in SCHEDULE:
        name, k = token[:-1], int(token[-1])
        if name in events:
            events[name](k)
        else:
            events[name[0]](name[1], k)

    for copies in staged.values():
        for copy, is_remote in copies:
            if not is_remote:
                copy.wait()
    for copy in returned:
        copy.wait_recv()
    for copy in started:
        if id(copy) not in sent:
            copy.wait_send()
    assert counts["remote"] <= N_REMOTE and counts["local"] <= N_LOCAL


def on_device(inputs, gate_pre, up_pre, grad_out, down_weight):
    any_spec = pl.BlockSpec(memory_space=pl.ANY)
    return pl.pallas_call(
        kernel,
        name="swiglu_backward",
        out_shape=(
            jax.ShapeDtypeStruct((D, FF), BF),
            jax.ShapeDtypeStruct((D, FF), BF),
            jax.ShapeDtypeStruct((FF, D), BF),
        ),
        in_specs=[any_spec] * 5,
        out_specs=(any_spec,) * 3,
        scratch_shapes=[
            pltpu.VMEM((2, TOK, D), BF),
            pltpu.VMEM((2, D, TOK), BF),
            pltpu.VMEM((8, 256, W), BF),
            pltpu.VMEM((8, 256, W), BF),
            pltpu.VMEM((8, 256, W), BF),
            pltpu.VMEM((8, 256, W), BF),
            pltpu.VMEM((4, 256, W), F32),
            pltpu.VMEM((2, 256, W), BF),
            pltpu.VMEM((2, 2, 256, W), BF),
            pltpu.VMEM((2, 256, NA - NS), BF),
            pltpu.VMEM((2, 256, NA - NS), BF),
            pltpu.VMEM((2, BW + NS // 2, D), BF),
            pltpu.VMEM((NA - NS, D), BF),
            pltpu.VMEM((W, TOK), BF),
            pltpu.VMEM((TOK, 256), BF),
            pltpu.VMEM((TOK, 256), BF),
            pltpu.VMEM((128, D), BF),
            pltpu.VMEM((D, 128), BF),
            pltpu.VMEM((2, 2, D, 256), BF),
            pltpu.VMEM((2, 2, D, 256), BF),
            pltpu.VMEM((2, 2, 256, D), BF),
            pltpu.SemaphoreType.DMA((N_REMOTE,)),
            pltpu.SemaphoreType.DMA((N_REMOTE,)),
            pltpu.SemaphoreType.DMA((N_LOCAL,)),
        ],
        compiler_params=pltpu.CompilerParams(
            collective_id=0, has_side_effects=True, vmem_limit_bytes=62 * 2**20
        ),
        cost_estimate=pl.CostEstimate(
            flops=8 * TOK * D * FF, bytes_accessed=40 * 2**20, transcendentals=TOK * FF
        ),
    )(inputs, gate_pre, up_pre, grad_out, down_weight)


def solution(mesh):
    placed = (P("row", "col"), P("col", "row"), P("col", "row"), P("row", "col"), P("row", "col"))
    return jax.shard_map(
        on_device,
        mesh=mesh,
        in_specs=placed,
        out_specs=(P("col", "row"), P("col", "row"), P("row", "col")),
        check_vma=False,
    )
```

```python
import functools

import jax
import jax.numpy as jnp
from jax import lax
from jax.experimental import pallas as pl
from jax.experimental.pallas import tpu as pltpu
from jax.sharding import PartitionSpec as P

MESH = pl.DeviceIdType.MESH
BF = jnp.bfloat16
F32 = jnp.float32

FF = 1664
D = 1024
TOK = 2048
B_CHUNKS = (256, 256)
S_CHUNKS = (256,)
A_CHUNKS = (256, 128)
BW = sum(B_CHUNKS)
NB = 2 * BW
NS = sum(S_CHUNKS)
NA = NS + sum(A_CHUNKS)
CHUNKS = B_CHUNKS + S_CHUNKS + A_CHUNKS
W = BW + NA
OFFS = tuple(sum(CHUNKS[:i]) for i in range(len(CHUNKS)))
NK = len(CHUNKS)
assert NB + NA == FF
FIRST_LATE = 3
LATE = sum(CHUNKS[FIRST_LATE:])
EARLY = FF - LATE
N_REMOTE = 166
N_LOCAL = 48


SCHEDULE = (
    "Zu4", "Au0", "Zu1", "Ag0", "gz0", "Au4", "Au1", "Zg1", "gr0", "Zg0",
    "Xg1", "Bu4", "Zu0", "Ag1", "Zg3", "Qg0", "iz0", "Zg2", "dz0", "Bu1",
    "Ag3", "Qu0", "Bg1", "Xg0", "Fg0", "Bg0", "Bu0", "ir0", "Fg1", "Ag2",
    "Lg0", "Eg0", "dw0", "P3", "H0", "H1", "Lg1", "Xi0", "P4", "R3",
    "Zu2", "R4", "Eg1", "dw1", "P0", "S3", "P1", "Zg4", "Zu3", "D1",
    "R0", "R1", "Fi0", "S0", "D0", "P2", "S4", "G0", "R2", "Li0",
    "S1", "S2", "Au2", "Au3", "Ei0", "O0", "Bg3", "G1", "Bu3", "Bu2",
    "Bg2", "T2", "O1", "Ag4", "H2", "D2", "G2", "H3", "T4", "Bg4",
    "D3", "T3", "O2", "G4", "H4", "G3", "D4", "O4", "O3",
)


def is_b(k):
    return k < len(B_CHUNKS)


def is_s(k):
    return len(B_CHUNKS) <= k < len(B_CHUNKS) + len(S_CHUNKS)


def rs_width(k):
    return CHUNKS[k] // 2 if is_s(k) else CHUNKS[k]


def kernel(
    x_hbm, gate_hbm, up_hbm, go_hbm, down_hbm,
    og_hbm, ou_hbm, od_hbm, xt_hbm, late_g, late_u, late_h,
    grad, in_t, gate, up, gh, part, kept, far, near, swap_s, swap_r, dn_b, dn_a,
    hid_t, gg, gu, x_in, x_t, st_g, st_u, st_d,
    send_sem, recv_sem, local_sem,
):
    r = lax.axis_index("row")
    c = lax.axis_index("col")
    x, zh, core = r // 4, (r // 2) % 2, r % 2
    zl, y = c // 4, c % 4
    z = zh * 2 + zl

    def dev(x_, y_, z_, core_):
        return (x_ * 4 + (z_ // 2) * 2 + core_, (z_ % 2) * 4 + y_)

    zo = dev(x, y, (1 - zh) * 2 + 1 - zl, core)
    xp, xm = (dev((x + d) % 4, y, z, core) for d in (1, 3))
    yp, ym = (dev(x, (y + d) % 4, z, core) for d in (1, 3))
    sib = dev(x, y, z, 1 - core)
    mate = dev(x, y, zh * 2 + 1 - zl, core)
    y_prev, y_next, y_far = (y + 3) % 4, (y + 1) % 4, (y + 2) % 4

    barrier = pltpu.get_barrier_semaphore()
    peers = (mate, zo, xp, xm, yp, ym, sib)
    for peer in peers:
        pl.semaphore_signal(barrier, inc=1, device_id=peer, device_id_type=MESH)

    counts = {"remote": 0, "local": 0}
    started = []
    sent = set()

    def send(src, dst, to):
        i = counts["remote"]
        counts["remote"] += 1
        copy = pltpu.make_async_remote_copy(
            src_ref=src, dst_ref=dst, send_sem=send_sem.at[i], recv_sem=recv_sem.at[i],
            device_id=to, device_id_type=MESH,
        )
        copy.start()
        started.append(copy)
        return copy

    def local(src, dst):
        i = counts["local"]
        counts["local"] += 1
        copy = pltpu.make_async_copy(src, dst, local_sem.at[i])
        copy.start()
        return copy

    def al(v, n):
        return pl.multiple_of(v, n)

    def token_block(x_, zh_):
        return al(((x_ % 2) * 8 + zh_ * 4 + (x_ // 2) * 2 + core) * 128, 128)

    own_tok = token_block(x, zh)

    def rows_of(buf, tok, lanes):
        return buf.at[:, :, pl.ds(tok, 128)] if lanes else buf.at[:, pl.ds(tok, 128)]

    def one_of(buf, tok, lanes):
        return buf.at[zl, :, pl.ds(tok, 128)] if lanes else buf.at[zl, pl.ds(tok, 128)]

    def cols(k):
        return pl.ds(OFFS[k], CHUNKS[k])

    def rcols(k):
        return pl.ds(OFFS[k], rs_width(k))

    def dn_at(k):
        return OFFS[k] if is_b(k) else BW + (OFFS[k] - BW) // 2

    def swap_cols(k):
        return pl.ds(OFFS[k] - BW - NS, CHUNKS[k])

    def out_at(k, plane):
        if is_b(k):
            return pl.ds(al(plane * BW + OFFS[k], 128), CHUNKS[k])
        return pl.ds(OFFS[k] + BW, CHUNKS[k])

    def down_parts(plane):
        parts = [(pl.ds(al(plane * BW, 128), BW), pl.ds(0, BW))]
        for k in range(NK):
            if is_s(k):
                n = CHUNKS[k] // 2
                parts.append((
                    pl.ds(al(BW + OFFS[k] + plane * n, 128), n),
                    pl.ds(dn_at(k), n),
                ))
        return parts

    in_copy = local(x_hbm, x_in)
    own_grad = local(go_hbm, one_of(grad, own_tok, False))
    streams = {"g": (gate_hbm, gate), "u": (up_hbm, up)}
    own_chunk = {}
    z_chunk = {}
    ya_c, yb_c = {}, {}

    def load_chunk(s, k):
        hbm, buf = streams[s]
        own_chunk[s, k] = local(hbm.at[:, out_at(k, zl)], buf.at[y * 2 + zl, :, cols(k)])

    def z_send_chunk(s, k):
        hbm, buf = streams[s]
        z_chunk[s, k] = send(hbm.at[:, out_at(k, 1 - zl)], buf.at[y * 2 + zl, :, cols(k)], mate)

    for k in range(NK):
        for s in "gu":
            load_chunk(s, k)
    dn_copies = [
        local(down_hbm.at[src], dn_b.at[zl, dst]) for src, dst in down_parts(zl)
    ]
    dn_copy_a = local(down_hbm.at[pl.ds(NB + NS, NA - NS)], dn_a)

    pl.semaphore_wait(barrier, len(peers))

    def gather_a(buf, k):
        sl = buf.at[pl.ds(y * 2, 2), :, cols(k)]
        return send(sl, sl, yp), send(sl, sl, ym)

    def gather_b(buf, k, first):
        first[0].wait_recv()
        lo = buf.at[y_prev * 2, :, cols(k)]
        one = send(lo, lo, yp)
        first[1].wait_recv()
        hi = buf.at[y_next * 2 + 1, :, cols(k)]
        return one, send(hi, hi, ym)

    def ya(s, k):
        hbm, buf = streams[s]
        if k == 0:
            dst = buf.at[y * 2 + zl, :, cols(k)]
            src = hbm.at[:, out_at(k, zl)]
            ya_c[s, k] = send(src, dst, yp), send(src, dst, ym)
            return
        own_chunk[s, k].wait()
        z_chunk[s, k].wait_recv()
        ya_c[s, k] = gather_a(buf, k)

    def yq(s, k):
        buf = streams[s][1]
        own_chunk[s, k].wait()
        z_chunk[s, k].wait_recv()
        other = buf.at[y * 2 + 1 - zl, :, cols(k)]
        ya_c[s, k] += send(other, other, yp), send(other, other, ym)

    def yb(s, k):
        buf = streams[s][1]
        if k == 0:
            own_p, own_m, other_p, other_m = ya_c[s, k]
            own_p.wait_recv()
            lo = buf.at[y_prev * 2 + zl, :, cols(k)]
            one = send(lo, lo, yp)
            other_m.wait_recv()
            hi = buf.at[y_next * 2 + 1 - zl, :, cols(k)]
            yb_c[s, k] = one, send(hi, hi, ym), own_m, other_p
            return
        yb_c[s, k] = gather_b(buf, k, ya_c[s, k])

    def yc(s, k):
        for copy in yb_c[s, k]:
            copy.wait_recv()

    def row_z(src, buf, lanes):
        dst = one_of(buf, own_tok, lanes)
        return [send(src, dst, to) for to in (mate, zo)]

    def row_z_relay(buf, lanes, copies):
        copies[0].wait_recv()
        tok = pl.ds(own_tok, 128)
        ref = buf.at[1 - zl, :, tok] if lanes else buf.at[1 - zl, tok]
        copies.append(send(ref, ref, zo))

    def block(buf, x_, q, which, lanes):
        tok = pl.ds(token_block((x + x_) % 4, q), 128)
        if which == "both":
            return buf.at[:, :, tok] if lanes else buf.at[:, tok]
        half = zl if which == "own" else 1 - zl
        return buf.at[half, :, tok] if lanes else buf.at[half, tok]

    class Row:
        def __init__(self, buf, which, lanes):
            self.buf, self.which, self.lanes = buf, which, lanes
            self.core = []

        def move(self, x_, q, to):
            ref = block(self.buf, x_, q, self.which, self.lanes)
            return send(ref, ref, to)

        def to_core(self, x_):
            self.core += [self.move(x_, q, sib) for q in range(2)]

        def first(self, waits):
            for wait in waits:
                wait()
            self.up = [self.move(0, q, xp) for q in range(2)]
            self.down = [self.move(0, q, xm) for q in range(2)]
            self.to_core(0)

        def relay(self):
            self.up[0].wait_recv()
            self.far = [self.move(3, 0, xp)]
            self.down[1].wait_recv()
            self.far.append(self.move(1, 1, xm))
            self.up[1].wait_recv()
            self.to_core(3)
            self.down[0].wait_recv()
            self.to_core(1)

        def last(self):
            for copy in self.far:
                copy.wait_recv()
            self.to_core(2)

        def done(self):
            for copy in self.core:
                copy.wait_recv()

    def silu_parts(t, k):
        g = gate[t, :, cols(k)].astype(F32)
        u = up[t, :, cols(k)].astype(F32)
        s = jax.nn.sigmoid(g)
        return g, u, s

    keep = []

    def keep_late(buf, hbm, k):
        at = pl.ds(OFFS[k] - OFFS[FIRST_LATE], CHUNKS[k])
        keep.append(local(buf.at[:, :, cols(k)], hbm.at[:, :, at]))

    def make_hidden(k):
        yc("g", k)
        yc("u", k)
        if k >= FIRST_LATE:
            keep_late(gate, late_g, k)
            keep_late(up, late_u, k)

        def body(t, carry):
            g, u, s = silu_parts(t, k)
            h = (g * s * u).astype(BF)
            hid_t[cols(k), pl.ds(al(t * 256, 256), 256)] = h.T
            return carry

        lax.fori_loop(0, 8, body, 0)

    def nt(a, b):
        return lax.dot_general(a, b, (((1,), (1,)), ((), ())), preferred_element_type=F32)

    def partial_block(k, t):
        n = rs_width(k)
        rows = pl.ds(al(t * 256, 256), 256)
        if is_b(k) or is_s(k):
            acc = nt(grad[0, rows], dn_b[0, pl.ds(dn_at(k), n)])
            return acc + nt(grad[1, rows], dn_b[1, pl.ds(dn_at(k), n)])
        return nt(grad[zl, rows], dn_a[pl.ds(OFFS[k] - BW - NS, n)])

    def make_sent(k):
        def body(i, carry):
            d = 2 - (i // 2) * (1 - 2 * (i % 2))
            t = ((y + d) % 4) * 2 + (i // 2 + i) % 2
            part[t, :, rcols(k)] = partial_block(k, t).astype(BF)
            return carry

        lax.fori_loop(0, 4, body, 0)

    def make_kept(k):
        def body(i, carry):
            d = (i // 2) * (1 + 2 * (i % 2))
            t = ((y + d) % 4) * 2 + i % 2
            kept[i, :, rcols(k)] = partial_block(k, t)
            return carry

        lax.fori_loop(0, 4, body, 0)

    rs1, rs2, swaps, ha, hb = {}, {}, {}, {}, {}

    def rs_a(k):
        make_sent(k)
        cc = rcols(k)
        rs1[k] = (
            send(part.at[y_far * 2, :, cc], far.at[0, :, cc], yp),
            send(part.at[y_far * 2 + 1, :, cc], far.at[1, :, cc], ym),
            send(part.at[y_next * 2 + 1, :, cc], near.at[0, 1, :, cc], yp),
            send(part.at[y_prev * 2, :, cc], near.at[1, 0, :, cc], ym),
        )
        make_kept(k)

    def rs_b(k):
        cc = rcols(k)
        rs1[k][0].wait_recv()
        part[y_next * 2, :, cc] = (kept[2, :, cc] + far[0, :, cc].astype(F32)).astype(BF)
        one = send(part.at[y_next * 2, :, cc], near.at[0, 0, :, cc], yp)
        rs1[k][1].wait_recv()
        part[y_prev * 2 + 1, :, cc] = (kept[3, :, cc] + far[1, :, cc].astype(F32)).astype(BF)
        rs2[k] = (one, send(part.at[y_prev * 2 + 1, :, cc], near.at[1, 1, :, cc], ym))

    def rs_c(k):
        cc = rcols(k)
        n = rs_width(k)
        for copy in (rs1[k][2], rs1[k][3], rs2[k][0], rs2[k][1]):
            copy.wait_recv()
        if is_s(k):
            to = pl.ds(al(OFFS[k] + zl * n, 128), n)
        elif is_b(k):
            to = cols(k)
        for q in range(2):
            a = kept[q, :, cc] + near[0, q, :, cc].astype(F32) + near[1, q, :, cc].astype(F32)
            if is_b(k) or is_s(k):
                gh[y * 2 + q, :, to] = a.astype(BF)
            else:
                kept[q, :, cc] = a
                swap_s[q, :, swap_cols(k)] = a.astype(BF)
        if is_b(k):
            ha[k] = gather_a(gh, k)
        elif is_s(k):
            ref = gh.at[pl.ds(y * 2, 2), :, to]
            swaps[k] = send(ref, ref, mate)
        else:
            swaps[k] = send(swap_s.at[:, :, swap_cols(k)], swap_r.at[:, :, swap_cols(k)], mate)

    def rs_d(k):
        swaps[k].wait_recv()
        if not is_s(k):
            for q in range(2):
                a = kept[q, :, cols(k)] + swap_r[q, :, swap_cols(k)].astype(F32)
                gh[y * 2 + q, :, cols(k)] = a.astype(BF)
        ha[k] = gather_a(gh, k)

    def hg_b(k):
        hb[k] = gather_b(gh, k, ha[k])

    staged = {}

    def halves(k):
        return (zl, 1 - zl) if is_b(k) else (zl,)

    def clear(kind, k):
        for copy, is_remote in staged.pop((kind, k - 2), ()):
            if is_remote:
                copy.wait_send()
                sent.add(id(copy))
            else:
                copy.wait()

    def ship(kind, k, st, out, by_rows):
        n = CHUNKS[k]
        p = k % 2
        res = []
        for i in range(len(halves(k))):
            src = st.at[p, i, pl.ds(0, n), :] if by_rows else st.at[p, i, :, pl.ds(0, n)]
            dst = out.at[out_at(k, zl), :] if by_rows else out.at[:, out_at(k, zl)]
            res.append((local(src, dst), False) if i == 0 else (send(src, dst, mate), True))
        staged[kind, k] = res

    returned = []

    def down_grad(k):
        clear("d", k)
        n = CHUNKS[k]
        p = k % 2

        def body(m, carry):
            w = pl.ds(al(m * 512, 512), 512)
            for i, h in enumerate(halves(k)):
                acc = jnp.dot(hid_t[cols(k), :], grad[h, :, w], preferred_element_type=F32)
                st_d[p, i, pl.ds(0, n), w] = acc.astype(BF)
            return carry

        lax.fori_loop(0, 2, body, 0)
        ship("d", k, st_d, od_hbm, True)
        returned.extend(copy for copy, is_remote in staged["d", k] if is_remote)

    def weight_grads(k):
        for copy in hb[k]:
            copy.wait_recv()
        if k >= FIRST_LATE:
            keep_late(gh, late_h, k)
            return
        clear("g", k)
        clear("u", k)
        n = CHUNKS[k]
        p = k % 2

        def elem(t, carry):
            g, u, s = silu_parts(t, k)
            e = gh[t, :, cols(k)].astype(F32)
            rows = pl.ds(al(t * 256, 256), 256)
            gu[rows, pl.ds(0, n)] = (e * (g * s)).astype(BF)
            gg[rows, pl.ds(0, n)] = (e * u * s * (1.0 + g * (1.0 - s))).astype(BF)
            return carry

        lax.fori_loop(0, 8, elem, 0)

        def body(m, carry):
            w = pl.ds(al(m * 1024, 1024), 1024)
            for i, h in enumerate(halves(k)):
                lhs = in_t[h, w, :]
                acc = jnp.dot(lhs, gg[:, pl.ds(0, n)], preferred_element_type=F32)
                st_g[p, i, w, pl.ds(0, n)] = acc.astype(BF)
                acc = jnp.dot(lhs, gu[:, pl.ds(0, n)], preferred_element_type=F32)
                st_u[p, i, w, pl.ds(0, n)] = acc.astype(BF)
            return carry

        lax.fori_loop(0, 1, body, 0)
        for kind, st, out in (("g", st_g, og_hbm), ("u", st_u, ou_hbm)):
            ship(kind, k, st, out, False)
            returned.extend(copy for copy, is_remote in staged[kind, k] if is_remote)

    rows = {
        "g0": Row(grad, "own", False),
        "g1": Row(grad, "other", False),
        "i0": Row(in_t, "both", True),
    }
    zs = {}

    def grad_z(k):
        zs["g"] = row_z(go_hbm, grad, False)

    def in_z(k):
        in_copy.wait()
        x_t[...] = x_in[...].T
        zs["own"] = local(x_t, one_of(in_t, own_tok, True))
        zs["i"] = row_z(x_t, in_t, True)

    def row_first(s, k):
        if s == "i":
            waits = [zs["own"].wait] + [copy.wait_recv for copy in zs["i"][1:]]
        elif k == 0:
            waits = [own_grad.wait, zs["g"][2].wait_recv]
        else:
            waits = [zs["g"][1].wait_recv]
        rows[s + str(k)].first(waits)

    def row_done(s, k):
        rows[s + str(k)].done()
        if s == "i":
            keep.append(local(in_t.at[zl], xt_hbm))

    def down_z(k):
        zs["d"] = [send(down_hbm.at[src], dn_b.at[zl, dst], mate) for src, dst in down_parts(1 - zl)]

    def down_done(k):
        if k == 0:
            dn_copy_a.wait()
        else:
            for copy in dn_copies:
                copy.wait()
            for copy in zs["d"]:
                copy.wait_recv()

    events = {
        "Z": z_send_chunk, "A": ya, "Q": yq, "B": yb,
        "X": row_first,
        "F": lambda s, k: rows[s + str(k)].relay(),
        "L": lambda s, k: rows[s + str(k)].last(),
        "E": row_done,
        "gr": lambda k: row_z_relay(grad, False, zs["g"]),
        "ir": lambda k: row_z_relay(in_t, True, zs["i"]),
        "gz": grad_z, "iz": in_z, "dz": down_z, "dw": down_done,
        "H": make_hidden, "P": rs_a, "R": rs_b, "S": rs_c, "T": rs_d, "G": hg_b,
        "D": down_grad, "O": weight_grads,
    }
    for token in SCHEDULE:
        name, k = token[:-1], int(token[-1])
        if name in events:
            events[name](k)
        else:
            events[name[0]](name[1], k)

    for copies in staged.values():
        for copy, is_remote in copies:
            if not is_remote:
                copy.wait()
    for copy in keep:
        copy.wait()
    for copy in returned:
        copy.wait_recv()
    for copy in started:
        if id(copy) not in sent:
            copy.wait_send()
    assert counts["remote"] <= N_REMOTE and counts["local"] <= N_LOCAL


def late_kernel(
    og_in, ou_in, od_in, xt_hbm, g_hbm, u_hbm, h_hbm,
    og, ou, od,
    xt, gate, up, gh, gg, gu, st_g, st_u, buf_g, buf_u, buf_d, sems,
):
    counts = [0]

    def move(src, dst):
        copy = pltpu.make_async_copy(src, dst, sems.at[counts[0]])
        counts[0] += 1
        return copy

    def run(copies):
        for copy in copies:
            copy.start()

    first = [move(h_hbm, gh), move(g_hbm, gate), move(u_hbm, up)]
    second = [move(xt_hbm, xt)]
    n = 2
    loads, stores = {}, {}
    early = pl.ds(0, EARLY)
    for name, src, buf, dst in (
        ("d", od_in, buf_d, od), ("g", og_in, buf_g, og), ("u", ou_in, buf_u, ou),
    ):
        part = src.shape[0] // n
        loads[name], stores[name] = [], []
        for j in range(n):
            rows = pl.ds(j * part, part)
            at = (rows, slice(None)) if name == "d" else (rows, early)
            loads[name].append(move(src.at[at], buf.at[rows]))
            stores[name].append(move(buf.at[rows], dst.at[at]))
    run(first)
    run(second)
    for name in "dgu":
        run(loads[name])
    for copy in first:
        copy.wait()

    def elem(t, carry):
        g = gate[t].astype(F32)
        u = up[t].astype(F32)
        e = gh[t].astype(F32)
        s = jax.nn.sigmoid(g)
        rows = pl.ds(pl.multiple_of(t * 256, 256), 256)
        gu[rows] = (e * (g * s)).astype(BF)
        gg[rows] = (e * u * s * (1.0 + g * (1.0 - s))).astype(BF)
        return carry

    def pass_on(name):
        for load, store in zip(loads[name], stores[name]):
            load.wait()
            store.start()

    def matmul(dst, rhs):
        def body(m, carry):
            w = pl.ds(pl.multiple_of(m * 512, 512), 512)
            dst[w] = jnp.dot(xt[w, :], rhs[...], preferred_element_type=F32).astype(BF)
            return carry

        lax.fori_loop(0, D // 512, body, 0)

    lax.fori_loop(0, 8, elem, 0)
    for copy in second:
        copy.wait()
    pass_on("d")
    matmul(st_g, gg)
    out_g = move(st_g, og.at[:, pl.ds(EARLY, LATE)])
    out_g.start()
    pass_on("g")
    pass_on("u")
    matmul(st_u, gu)
    out_u = move(st_u, ou.at[:, pl.ds(EARLY, LATE)])
    out_u.start()
    for name in "dgu":
        for store in stores[name]:
            store.wait()
    out_g.wait()
    out_u.wait()


def finish(og, ou, od, xt, g, u, h):
    any_spec = pl.BlockSpec(memory_space=pl.ANY)
    return pl.pallas_call(
        late_kernel,
        name="late_grads",
        out_shape=tuple(jax.ShapeDtypeStruct(a.shape, a.dtype) for a in (og, ou, od)),
        in_specs=[any_spec] * 7,
        out_specs=(any_spec,) * 3,
        scratch_shapes=[
            pltpu.VMEM((D, TOK), BF),
            pltpu.VMEM((8, 256, LATE), BF),
            pltpu.VMEM((8, 256, LATE), BF),
            pltpu.VMEM((8, 256, LATE), BF),
            pltpu.VMEM((TOK, LATE), BF),
            pltpu.VMEM((TOK, LATE), BF),
            pltpu.VMEM((D, LATE), BF),
            pltpu.VMEM((D, LATE), BF),
            pltpu.VMEM((D, EARLY), BF),
            pltpu.VMEM((D, EARLY), BF),
            pltpu.VMEM((FF, D), BF),
            pltpu.SemaphoreType.DMA((24,)),
        ],
        compiler_params=pltpu.CompilerParams(vmem_limit_bytes=62 * 2**20),
        cost_estimate=pl.CostEstimate(
            flops=4 * TOK * D * LATE, bytes_accessed=28 * 2**20, transcendentals=TOK * LATE
        ),
    )(og, ou, od, xt, g, u, h)


def on_device(inputs, gate_pre, up_pre, grad_out, down_weight):
    any_spec = pl.BlockSpec(memory_space=pl.ANY)
    return finish(*pl.pallas_call(
        kernel,
        name="swiglu_backward",
        out_shape=(
            jax.ShapeDtypeStruct((D, FF), BF),
            jax.ShapeDtypeStruct((D, FF), BF),
            jax.ShapeDtypeStruct((FF, D), BF),
            jax.ShapeDtypeStruct((D, TOK), BF),
            jax.ShapeDtypeStruct((8, 256, LATE), BF),
            jax.ShapeDtypeStruct((8, 256, LATE), BF),
            jax.ShapeDtypeStruct((8, 256, LATE), BF),
        ),
        in_specs=[any_spec] * 5,
        out_specs=(any_spec,) * 7,
        scratch_shapes=[
            pltpu.VMEM((2, TOK, D), BF),
            pltpu.VMEM((2, D, TOK), BF),
            pltpu.VMEM((8, 256, W), BF),
            pltpu.VMEM((8, 256, W), BF),
            pltpu.VMEM((8, 256, W), BF),
            pltpu.VMEM((8, 256, W), BF),
            pltpu.VMEM((4, 256, W), F32),
            pltpu.VMEM((2, 256, W), BF),
            pltpu.VMEM((2, 2, 256, W), BF),
            pltpu.VMEM((2, 256, NA - NS), BF),
            pltpu.VMEM((2, 256, NA - NS), BF),
            pltpu.VMEM((2, BW + NS // 2, D), BF),
            pltpu.VMEM((NA - NS, D), BF),
            pltpu.VMEM((W, TOK), BF),
            pltpu.VMEM((TOK, 256), BF),
            pltpu.VMEM((TOK, 256), BF),
            pltpu.VMEM((128, D), BF),
            pltpu.VMEM((D, 128), BF),
            pltpu.VMEM((2, 2, D, 256), BF),
            pltpu.VMEM((2, 2, D, 256), BF),
            pltpu.VMEM((2, 2, 256, D), BF),
            pltpu.SemaphoreType.DMA((N_REMOTE,)),
            pltpu.SemaphoreType.DMA((N_REMOTE,)),
            pltpu.SemaphoreType.DMA((N_LOCAL,)),
        ],
        compiler_params=pltpu.CompilerParams(
            collective_id=0, has_side_effects=True, vmem_limit_bytes=62 * 2**20
        ),
        cost_estimate=pl.CostEstimate(
            flops=8 * TOK * D * FF, bytes_accessed=40 * 2**20, transcendentals=TOK * FF
        ),
    )(inputs, gate_pre, up_pre, grad_out, down_weight))


def solution(mesh):
    placed = (P("row", "col"), P("col", "row"), P("col", "row"), P("row", "col"), P("row", "col"))
    return jax.shard_map(
        on_device,
        mesh=mesh,
        in_specs=placed,
        out_specs=(P("col", "row"), P("col", "row"), P("row", "col")),
        check_vma=False,
    )
```

```python
import functools

import jax
import jax.numpy as jnp
from jax import lax
from jax.experimental import pallas as pl
from jax.experimental.pallas import tpu as pltpu
from jax.sharding import PartitionSpec as P

MESH = pl.DeviceIdType.MESH
BF = jnp.bfloat16
F32 = jnp.float32

FF = 1664
D = 1024
TOK = 2048
B_CHUNKS = (256, 256)
S_CHUNKS = (256,)
A_CHUNKS = (256, 128)
BW = sum(B_CHUNKS)
NB = 2 * BW
NS = sum(S_CHUNKS)
NA = NS + sum(A_CHUNKS)
CHUNKS = B_CHUNKS + S_CHUNKS + A_CHUNKS
W = BW + NA
OFFS = tuple(sum(CHUNKS[:i]) for i in range(len(CHUNKS)))
NK = len(CHUNKS)
assert NB + NA == FF
FIRST_LATE = 3
LATE = sum(CHUNKS[FIRST_LATE:])
EARLY = FF - LATE
N_REMOTE = 166
N_LOCAL = 48


SCHEDULE = (
    "Zg1", "gz0", "Ag0", "Au0", "Ag1", "Zg4", "Zu1", "gr0", "Zu2", "Xg1",
    "Zu0", "Ag4", "Au1", "Zu3", "Bg4", "Zg0", "iz0", "dz0", "Qu0", "Xg0",
    "Au2", "Au3", "Bu0", "Qg0", "Fg0", "Bu1", "ir0", "Fg1", "Bg1", "Bg0",
    "Lg0", "Eg0", "dw0", "P4", "Lg1", "Xi0", "P3", "H1", "Zg2", "Eg1",
    "dw1", "P2", "P0", "H0", "Zg3", "R3", "D1", "R0", "R2", "P1",
    "S0", "Fi0", "Zu4", "S2", "S3", "D0", "R1", "R4", "G0", "Li0",
    "S1", "Au4", "S4", "Ag3", "Ei0", "O0", "Ag2", "G1", "Bg3", "Bg2",
    "Bu3", "T2", "Bu2", "Bu4", "O1", "T3", "H2", "T4", "H3", "G2",
    "D2", "H4", "D3", "G3", "D4", "G4", "O2", "O3", "O4",
)


def is_b(k):
    return k < len(B_CHUNKS)


def is_s(k):
    return len(B_CHUNKS) <= k < len(B_CHUNKS) + len(S_CHUNKS)


def rs_width(k):
    return CHUNKS[k] // 2 if is_s(k) else CHUNKS[k]


def kernel(
    x_hbm, gate_hbm, up_hbm, go_hbm, down_hbm,
    og_hbm, ou_hbm, od_hbm, xt_hbm, late_g, late_u, late_h,
    grad, in_t, gate, up, gh, part, kept, far, near, swap_s, swap_r, dn_b, dn_a,
    hid_t, gg, gu, x_in, x_t, st_g, st_u, st_d,
    send_sem, recv_sem, local_sem,
):
    r = lax.axis_index("row")
    c = lax.axis_index("col")
    x, zh, core = r // 4, (r // 2) % 2, r % 2
    zl, y = c // 4, c % 4
    z = zh * 2 + zl

    def dev(x_, y_, z_, core_):
        return (x_ * 4 + (z_ // 2) * 2 + core_, (z_ % 2) * 4 + y_)

    zo = dev(x, y, (1 - zh) * 2 + 1 - zl, core)
    xp, xm = (dev((x + d) % 4, y, z, core) for d in (1, 3))
    yp, ym = (dev(x, (y + d) % 4, z, core) for d in (1, 3))
    sib = dev(x, y, z, 1 - core)
    mate = dev(x, y, zh * 2 + 1 - zl, core)
    y_prev, y_next, y_far = (y + 3) % 4, (y + 1) % 4, (y + 2) % 4

    barrier = pltpu.get_barrier_semaphore()
    peers = (mate, zo, xp, xm, yp, ym, sib)
    for peer in peers:
        pl.semaphore_signal(barrier, inc=1, device_id=peer, device_id_type=MESH)

    counts = {"remote": 0, "local": 0}
    started = []
    sent = set()

    def send(src, dst, to):
        i = counts["remote"]
        counts["remote"] += 1
        copy = pltpu.make_async_remote_copy(
            src_ref=src, dst_ref=dst, send_sem=send_sem.at[i], recv_sem=recv_sem.at[i],
            device_id=to, device_id_type=MESH,
        )
        copy.start()
        started.append(copy)
        return copy

    def local(src, dst):
        i = counts["local"]
        counts["local"] += 1
        copy = pltpu.make_async_copy(src, dst, local_sem.at[i])
        copy.start()
        return copy

    def al(v, n):
        return pl.multiple_of(v, n)

    def token_block(x_, zh_):
        return al(((x_ % 2) * 8 + zh_ * 4 + (x_ // 2) * 2 + core) * 128, 128)

    own_tok = token_block(x, zh)

    def rows_of(buf, tok, lanes):
        return buf.at[:, :, pl.ds(tok, 128)] if lanes else buf.at[:, pl.ds(tok, 128)]

    def one_of(buf, tok, lanes):
        return buf.at[zl, :, pl.ds(tok, 128)] if lanes else buf.at[zl, pl.ds(tok, 128)]

    def cols(k):
        return pl.ds(OFFS[k], CHUNKS[k])

    def rcols(k):
        return pl.ds(OFFS[k], rs_width(k))

    def dn_at(k):
        return OFFS[k] if is_b(k) else BW + (OFFS[k] - BW) // 2

    def swap_cols(k):
        return pl.ds(OFFS[k] - BW - NS, CHUNKS[k])

    def out_at(k, plane):
        if is_b(k):
            return pl.ds(al(plane * BW + OFFS[k], 128), CHUNKS[k])
        return pl.ds(OFFS[k] + BW, CHUNKS[k])

    def down_parts(plane):
        parts = [(pl.ds(al(plane * BW, 128), BW), pl.ds(0, BW))]
        for k in range(NK):
            if is_s(k):
                n = CHUNKS[k] // 2
                parts.append((
                    pl.ds(al(BW + OFFS[k] + plane * n, 128), n),
                    pl.ds(dn_at(k), n),
                ))
        return parts

    in_copy = local(x_hbm, x_in)
    own_grad = local(go_hbm, one_of(grad, own_tok, False))
    streams = {"g": (gate_hbm, gate), "u": (up_hbm, up)}
    own_chunk = {}
    z_chunk = {}
    ya_c, yb_c = {}, {}

    def load_chunk(s, k):
        hbm, buf = streams[s]
        own_chunk[s, k] = local(hbm.at[:, out_at(k, zl)], buf.at[y * 2 + zl, :, cols(k)])

    def z_send_chunk(s, k):
        hbm, buf = streams[s]
        z_chunk[s, k] = send(hbm.at[:, out_at(k, 1 - zl)], buf.at[y * 2 + zl, :, cols(k)], mate)

    for k in range(NK):
        for s in "gu":
            load_chunk(s, k)
    dn_copies = [
        local(down_hbm.at[src], dn_b.at[zl, dst]) for src, dst in down_parts(zl)
    ]
    dn_copy_a = local(down_hbm.at[pl.ds(NB + NS, NA - NS)], dn_a)

    pl.semaphore_wait(barrier, len(peers))

    def gather_a(buf, k):
        sl = buf.at[pl.ds(y * 2, 2), :, cols(k)]
        return send(sl, sl, yp), send(sl, sl, ym)

    def gather_b(buf, k, first):
        first[0].wait_recv()
        lo = buf.at[y_prev * 2, :, cols(k)]
        one = send(lo, lo, yp)
        first[1].wait_recv()
        hi = buf.at[y_next * 2 + 1, :, cols(k)]
        return one, send(hi, hi, ym)

    def ya(s, k):
        hbm, buf = streams[s]
        if k == 0:
            dst = buf.at[y * 2 + zl, :, cols(k)]
            src = hbm.at[:, out_at(k, zl)]
            ya_c[s, k] = send(src, dst, yp), send(src, dst, ym)
            return
        own_chunk[s, k].wait()
        z_chunk[s, k].wait_recv()
        ya_c[s, k] = gather_a(buf, k)

    def yq(s, k):
        buf = streams[s][1]
        own_chunk[s, k].wait()
        z_chunk[s, k].wait_recv()
        other = buf.at[y * 2 + 1 - zl, :, cols(k)]
        ya_c[s, k] += send(other, other, yp), send(other, other, ym)

    def yb(s, k):
        buf = streams[s][1]
        if k == 0:
            own_p, own_m, other_p, other_m = ya_c[s, k]
            own_p.wait_recv()
            lo = buf.at[y_prev * 2 + zl, :, cols(k)]
            one = send(lo, lo, yp)
            other_m.wait_recv()
            hi = buf.at[y_next * 2 + 1 - zl, :, cols(k)]
            yb_c[s, k] = one, send(hi, hi, ym), own_m, other_p
            return
        yb_c[s, k] = gather_b(buf, k, ya_c[s, k])

    def yc(s, k):
        for copy in yb_c[s, k]:
            copy.wait_recv()

    def row_z(src, buf, lanes):
        dst = one_of(buf, own_tok, lanes)
        return [send(src, dst, to) for to in (mate, zo)]

    def row_z_relay(buf, lanes, copies):
        copies[0].wait_recv()
        tok = pl.ds(own_tok, 128)
        ref = buf.at[1 - zl, :, tok] if lanes else buf.at[1 - zl, tok]
        copies.append(send(ref, ref, zo))

    def block(buf, x_, q, which, lanes):
        tok = pl.ds(token_block((x + x_) % 4, q), 128)
        if which == "both":
            return buf.at[:, :, tok] if lanes else buf.at[:, tok]
        half = zl if which == "own" else 1 - zl
        return buf.at[half, :, tok] if lanes else buf.at[half, tok]

    class Row:
        def __init__(self, buf, which, lanes):
            self.buf, self.which, self.lanes = buf, which, lanes
            self.core = []

        def move(self, x_, q, to):
            ref = block(self.buf, x_, q, self.which, self.lanes)
            return send(ref, ref, to)

        def to_core(self, x_):
            self.core += [self.move(x_, q, sib) for q in range(2)]

        def first(self, waits):
            for wait in waits:
                wait()
            self.up = [self.move(0, q, xp) for q in range(2)]
            self.down = [self.move(0, q, xm) for q in range(2)]
            self.to_core(0)

        def relay(self):
            self.up[0].wait_recv()
            self.far = [self.move(3, 0, xp)]
            self.down[1].wait_recv()
            self.far.append(self.move(1, 1, xm))
            self.up[1].wait_recv()
            self.to_core(3)
            self.down[0].wait_recv()
            self.to_core(1)

        def last(self):
            for copy in self.far:
                copy.wait_recv()
            self.to_core(2)

        def done(self):
            for copy in self.core:
                copy.wait_recv()

    def silu_parts(t, k):
        g = gate[t, :, cols(k)].astype(F32)
        u = up[t, :, cols(k)].astype(F32)
        s = jax.nn.sigmoid(g)
        return g, u, s

    keep = []

    def keep_late(buf, hbm, k):
        at = pl.ds(OFFS[k] - OFFS[FIRST_LATE], CHUNKS[k])
        keep.append(local(buf.at[:, :, cols(k)], hbm.at[:, :, at]))

    def make_hidden(k):
        yc("g", k)
        yc("u", k)
        if k >= FIRST_LATE:
            keep_late(gate, late_g, k)
            keep_late(up, late_u, k)

        def body(t, carry):
            g, u, s = silu_parts(t, k)
            h = (g * s * u).astype(BF)
            hid_t[cols(k), pl.ds(al(t * 256, 256), 256)] = h.T
            return carry

        lax.fori_loop(0, 8, body, 0)

    def nt(a, b):
        return lax.dot_general(a, b, (((1,), (1,)), ((), ())), preferred_element_type=F32)

    def partial_blocks(k, blocks):
        n = rs_width(k)

        def lhs(h):
            return jnp.concatenate([grad[h, pl.ds(al(t * 256, 256), 256)] for t in blocks], axis=0)

        if is_b(k) or is_s(k):
            acc = nt(lhs(0), dn_b[0, pl.ds(dn_at(k), n)])
            return acc + nt(lhs(1), dn_b[1, pl.ds(dn_at(k), n)])
        return nt(lhs(zl), dn_a[pl.ds(OFFS[k] - BW - NS, n)])

    def make_sent(k):
        blocks = (y_far * 2, y_far * 2 + 1, y_next * 2 + 1, y_prev * 2)
        acc = partial_blocks(k, blocks)
        for i, t in enumerate(blocks):
            part[t, :, rcols(k)] = acc[i * 256:(i + 1) * 256].astype(BF)

    def make_kept(k):
        acc = partial_blocks(k, (y * 2, y * 2 + 1, y_next * 2, y_prev * 2 + 1))
        for i in range(4):
            kept[i, :, rcols(k)] = acc[i * 256:(i + 1) * 256]

    rs1, rs2, swaps, ha, hb = {}, {}, {}, {}, {}

    def rs_a(k):
        make_sent(k)
        cc = rcols(k)
        rs1[k] = (
            send(part.at[y_far * 2, :, cc], far.at[0, :, cc], yp),
            send(part.at[y_far * 2 + 1, :, cc], far.at[1, :, cc], ym),
            send(part.at[y_next * 2 + 1, :, cc], near.at[0, 1, :, cc], yp),
            send(part.at[y_prev * 2, :, cc], near.at[1, 0, :, cc], ym),
        )
        make_kept(k)

    def rs_b(k):
        cc = rcols(k)
        rs1[k][0].wait_recv()
        part[y_next * 2, :, cc] = (kept[2, :, cc] + far[0, :, cc].astype(F32)).astype(BF)
        one = send(part.at[y_next * 2, :, cc], near.at[0, 0, :, cc], yp)
        rs1[k][1].wait_recv()
        part[y_prev * 2 + 1, :, cc] = (kept[3, :, cc] + far[1, :, cc].astype(F32)).astype(BF)
        rs2[k] = (one, send(part.at[y_prev * 2 + 1, :, cc], near.at[1, 1, :, cc], ym))

    def rs_c(k):
        cc = rcols(k)
        n = rs_width(k)
        for copy in (rs1[k][2], rs1[k][3], rs2[k][0], rs2[k][1]):
            copy.wait_recv()
        if is_s(k):
            to = pl.ds(al(OFFS[k] + zl * n, 128), n)
        elif is_b(k):
            to = cols(k)
        for q in range(2):
            a = kept[q, :, cc] + near[0, q, :, cc].astype(F32) + near[1, q, :, cc].astype(F32)
            if is_b(k) or is_s(k):
                gh[y * 2 + q, :, to] = a.astype(BF)
            else:
                kept[q, :, cc] = a
                swap_s[q, :, swap_cols(k)] = a.astype(BF)
        if is_b(k):
            ha[k] = gather_a(gh, k)
        elif is_s(k):
            ref = gh.at[pl.ds(y * 2, 2), :, to]
            swaps[k] = send(ref, ref, mate)
        else:
            swaps[k] = send(swap_s.at[:, :, swap_cols(k)], swap_r.at[:, :, swap_cols(k)], mate)

    def rs_d(k):
        swaps[k].wait_recv()
        if not is_s(k):
            for q in range(2):
                a = kept[q, :, cols(k)] + swap_r[q, :, swap_cols(k)].astype(F32)
                gh[y * 2 + q, :, cols(k)] = a.astype(BF)
        ha[k] = gather_a(gh, k)

    def hg_b(k):
        hb[k] = gather_b(gh, k, ha[k])

    staged = {}

    def halves(k):
        return (zl, 1 - zl) if is_b(k) else (zl,)

    def clear(kind, k):
        for copy, is_remote in staged.pop((kind, k - 2), ()):
            if is_remote:
                copy.wait_send()
                sent.add(id(copy))
            else:
                copy.wait()

    def ship(kind, k, st, out, by_rows):
        n = CHUNKS[k]
        p = k % 2
        res = []
        for i in range(len(halves(k))):
            src = st.at[p, i, pl.ds(0, n), :] if by_rows else st.at[p, i, :, pl.ds(0, n)]
            dst = out.at[out_at(k, zl), :] if by_rows else out.at[:, out_at(k, zl)]
            res.append((local(src, dst), False) if i == 0 else (send(src, dst, mate), True))
        staged[kind, k] = res

    returned = []

    def down_grad(k):
        clear("d", k)
        n = CHUNKS[k]
        p = k % 2

        def body(m, carry):
            w = pl.ds(al(m * 512, 512), 512)
            for i, h in enumerate(halves(k)):
                acc = jnp.dot(hid_t[cols(k), :], grad[h, :, w], preferred_element_type=F32)
                st_d[p, i, pl.ds(0, n), w] = acc.astype(BF)
            return carry

        lax.fori_loop(0, 2, body, 0)
        ship("d", k, st_d, od_hbm, True)
        returned.extend(copy for copy, is_remote in staged["d", k] if is_remote)

    def weight_grads(k):
        for copy in hb[k]:
            copy.wait_recv()
        if k >= FIRST_LATE:
            keep_late(gh, late_h, k)
            return
        clear("g", k)
        clear("u", k)
        n = CHUNKS[k]
        p = k % 2

        def elem(t, carry):
            g, u, s = silu_parts(t, k)
            e = gh[t, :, cols(k)].astype(F32)
            rows = pl.ds(al(t * 256, 256), 256)
            gu[rows, pl.ds(0, n)] = (e * (g * s)).astype(BF)
            gg[rows, pl.ds(0, n)] = (e * u * s * (1.0 + g * (1.0 - s))).astype(BF)
            return carry

        lax.fori_loop(0, 8, elem, 0)

        def body(m, carry):
            w = pl.ds(al(m * 1024, 1024), 1024)
            for i, h in enumerate(halves(k)):
                lhs = in_t[h, w, :]
                acc = jnp.dot(lhs, gg[:, pl.ds(0, n)], preferred_element_type=F32)
                st_g[p, i, w, pl.ds(0, n)] = acc.astype(BF)
                acc = jnp.dot(lhs, gu[:, pl.ds(0, n)], preferred_element_type=F32)
                st_u[p, i, w, pl.ds(0, n)] = acc.astype(BF)
            return carry

        lax.fori_loop(0, 1, body, 0)
        for kind, st, out in (("g", st_g, og_hbm), ("u", st_u, ou_hbm)):
            ship(kind, k, st, out, False)
            returned.extend(copy for copy, is_remote in staged[kind, k] if is_remote)

    rows = {
        "g0": Row(grad, "own", False),
        "g1": Row(grad, "other", False),
        "i0": Row(in_t, "both", True),
    }
    zs = {}

    def grad_z(k):
        zs["g"] = row_z(go_hbm, grad, False)

    def in_z(k):
        in_copy.wait()
        x_t[...] = x_in[...].T
        zs["own"] = local(x_t, one_of(in_t, own_tok, True))
        zs["i"] = row_z(x_t, in_t, True)

    def row_first(s, k):
        if s == "i":
            waits = [zs["own"].wait] + [copy.wait_recv for copy in zs["i"][1:]]
        elif k == 0:
            waits = [own_grad.wait, zs["g"][2].wait_recv]
        else:
            waits = [zs["g"][1].wait_recv]
        rows[s + str(k)].first(waits)

    def row_done(s, k):
        rows[s + str(k)].done()
        if s == "i":
            keep.append(local(in_t.at[zl], xt_hbm))

    def down_z(k):
        zs["d"] = [send(down_hbm.at[src], dn_b.at[zl, dst], mate) for src, dst in down_parts(1 - zl)]

    def down_done(k):
        if k == 0:
            dn_copy_a.wait()
        else:
            for copy in dn_copies:
                copy.wait()
            for copy in zs["d"]:
                copy.wait_recv()

    events = {
        "Z": z_send_chunk, "A": ya, "Q": yq, "B": yb,
        "X": row_first,
        "F": lambda s, k: rows[s + str(k)].relay(),
        "L": lambda s, k: rows[s + str(k)].last(),
        "E": row_done,
        "gr": lambda k: row_z_relay(grad, False, zs["g"]),
        "ir": lambda k: row_z_relay(in_t, True, zs["i"]),
        "gz": grad_z, "iz": in_z, "dz": down_z, "dw": down_done,
        "H": make_hidden, "P": rs_a, "R": rs_b, "S": rs_c, "T": rs_d, "G": hg_b,
        "D": down_grad, "O": weight_grads,
    }
    for token in SCHEDULE:
        name, k = token[:-1], int(token[-1])
        if name in events:
            events[name](k)
        else:
            events[name[0]](name[1], k)

    for copies in staged.values():
        for copy, is_remote in copies:
            if not is_remote:
                copy.wait()
    for copy in keep:
        copy.wait()
    for copy in returned:
        copy.wait_recv()
    for copy in started:
        if id(copy) not in sent:
            copy.wait_send()
    assert counts["remote"] <= N_REMOTE and counts["local"] <= N_LOCAL


def late_kernel(
    og_in, ou_in, od_in, xt_hbm, g_hbm, u_hbm, h_hbm,
    og, ou, od,
    xt, gate, up, gh, gg, gu, st_g, st_u, buf_g, buf_u, buf_d, sems,
):
    counts = [0]

    def move(src, dst):
        copy = pltpu.make_async_copy(src, dst, sems.at[counts[0]])
        counts[0] += 1
        return copy

    def run(copies):
        for copy in copies:
            copy.start()

    first = [move(h_hbm, gh), move(g_hbm, gate), move(u_hbm, up)]
    second = [move(xt_hbm, xt)]
    n = 2
    loads, stores = {}, {}
    early = pl.ds(0, EARLY)
    for name, src, buf, dst in (
        ("d", od_in, buf_d, od), ("g", og_in, buf_g, og), ("u", ou_in, buf_u, ou),
    ):
        part = src.shape[0] // n
        loads[name], stores[name] = [], []
        for j in range(n):
            rows = pl.ds(j * part, part)
            at = (rows, slice(None)) if name == "d" else (rows, early)
            loads[name].append(move(src.at[at], buf.at[rows]))
            stores[name].append(move(buf.at[rows], dst.at[at]))
    run(first)
    run(second)
    for name in "dgu":
        run(loads[name])
    for copy in first:
        copy.wait()

    def elem(t, carry):
        g = gate[t].astype(F32)
        u = up[t].astype(F32)
        e = gh[t].astype(F32)
        s = jax.nn.sigmoid(g)
        rows = pl.ds(pl.multiple_of(t * 256, 256), 256)
        gu[rows] = (e * (g * s)).astype(BF)
        gg[rows] = (e * u * s * (1.0 + g * (1.0 - s))).astype(BF)
        return carry

    def pass_on(name):
        for load, store in zip(loads[name], stores[name]):
            load.wait()
            store.start()

    def matmul(dst, rhs):
        def body(m, carry):
            w = pl.ds(pl.multiple_of(m * 512, 512), 512)
            dst[w] = jnp.dot(xt[w, :], rhs[...], preferred_element_type=F32).astype(BF)
            return carry

        lax.fori_loop(0, D // 512, body, 0)

    lax.fori_loop(0, 8, elem, 0)
    for copy in second:
        copy.wait()
    pass_on("d")
    matmul(st_g, gg)
    out_g = move(st_g, og.at[:, pl.ds(EARLY, LATE)])
    out_g.start()
    pass_on("g")
    pass_on("u")
    matmul(st_u, gu)
    out_u = move(st_u, ou.at[:, pl.ds(EARLY, LATE)])
    out_u.start()
    for name in "dgu":
        for store in stores[name]:
            store.wait()
    out_g.wait()
    out_u.wait()


def finish(og, ou, od, xt, g, u, h):
    any_spec = pl.BlockSpec(memory_space=pl.ANY)
    return pl.pallas_call(
        late_kernel,
        name="late_grads",
        out_shape=tuple(jax.ShapeDtypeStruct(a.shape, a.dtype) for a in (og, ou, od)),
        in_specs=[any_spec] * 7,
        out_specs=(any_spec,) * 3,
        scratch_shapes=[
            pltpu.VMEM((D, TOK), BF),
            pltpu.VMEM((8, 256, LATE), BF),
            pltpu.VMEM((8, 256, LATE), BF),
            pltpu.VMEM((8, 256, LATE), BF),
            pltpu.VMEM((TOK, LATE), BF),
            pltpu.VMEM((TOK, LATE), BF),
            pltpu.VMEM((D, LATE), BF),
            pltpu.VMEM((D, LATE), BF),
            pltpu.VMEM((D, EARLY), BF),
            pltpu.VMEM((D, EARLY), BF),
            pltpu.VMEM((FF, D), BF),
            pltpu.SemaphoreType.DMA((24,)),
        ],
        compiler_params=pltpu.CompilerParams(vmem_limit_bytes=62 * 2**20),
        cost_estimate=pl.CostEstimate(
            flops=4 * TOK * D * LATE, bytes_accessed=28 * 2**20, transcendentals=TOK * LATE
        ),
    )(og, ou, od, xt, g, u, h)


def on_device(inputs, gate_pre, up_pre, grad_out, down_weight):
    any_spec = pl.BlockSpec(memory_space=pl.ANY)
    return finish(*pl.pallas_call(
        kernel,
        name="swiglu_backward",
        out_shape=(
            jax.ShapeDtypeStruct((D, FF), BF),
            jax.ShapeDtypeStruct((D, FF), BF),
            jax.ShapeDtypeStruct((FF, D), BF),
            jax.ShapeDtypeStruct((D, TOK), BF),
            jax.ShapeDtypeStruct((8, 256, LATE), BF),
            jax.ShapeDtypeStruct((8, 256, LATE), BF),
            jax.ShapeDtypeStruct((8, 256, LATE), BF),
        ),
        in_specs=[any_spec] * 5,
        out_specs=(any_spec,) * 7,
        scratch_shapes=[
            pltpu.VMEM((2, TOK, D), BF),
            pltpu.VMEM((2, D, TOK), BF),
            pltpu.VMEM((8, 256, W), BF),
            pltpu.VMEM((8, 256, W), BF),
            pltpu.VMEM((8, 256, W), BF),
            pltpu.VMEM((8, 256, W), BF),
            pltpu.VMEM((4, 256, W), F32),
            pltpu.VMEM((2, 256, W), BF),
            pltpu.VMEM((2, 2, 256, W), BF),
            pltpu.VMEM((2, 256, NA - NS), BF),
            pltpu.VMEM((2, 256, NA - NS), BF),
            pltpu.VMEM((2, BW + NS // 2, D), BF),
            pltpu.VMEM((NA - NS, D), BF),
            pltpu.VMEM((W, TOK), BF),
            pltpu.VMEM((TOK, 256), BF),
            pltpu.VMEM((TOK, 256), BF),
            pltpu.VMEM((128, D), BF),
            pltpu.VMEM((D, 128), BF),
            pltpu.VMEM((2, 2, D, 256), BF),
            pltpu.VMEM((2, 2, D, 256), BF),
            pltpu.VMEM((2, 2, 256, D), BF),
            pltpu.SemaphoreType.DMA((N_REMOTE,)),
            pltpu.SemaphoreType.DMA((N_REMOTE,)),
            pltpu.SemaphoreType.DMA((N_LOCAL,)),
        ],
        compiler_params=pltpu.CompilerParams(
            collective_id=0, has_side_effects=True, vmem_limit_bytes=62 * 2**20
        ),
        cost_estimate=pl.CostEstimate(
            flops=8 * TOK * D * FF, bytes_accessed=40 * 2**20, transcendentals=TOK * FF
        ),
    )(inputs, gate_pre, up_pre, grad_out, down_weight))


def solution(mesh):
    placed = (P("row", "col"), P("col", "row"), P("col", "row"), P("row", "col"), P("row", "col"))
    return jax.shard_map(
        on_device,
        mesh=mesh,
        in_specs=placed,
        out_specs=(P("col", "row"), P("col", "row"), P("row", "col")),
        check_vma=False,
    )
```

```python
import functools

import jax
import jax.numpy as jnp
from jax import lax
from jax.experimental import pallas as pl
from jax.experimental.pallas import tpu as pltpu
from jax.sharding import PartitionSpec as P

MESH = pl.DeviceIdType.MESH
BF = jnp.bfloat16
F32 = jnp.float32

FF = 1664
D = 1024
TOK = 2048
B_CHUNKS = (256, 256)
S_CHUNKS = (256,)
A_CHUNKS = (256, 128)
BW = sum(B_CHUNKS)
NB = 2 * BW
NS = sum(S_CHUNKS)
NA = NS + sum(A_CHUNKS)
CHUNKS = B_CHUNKS + S_CHUNKS + A_CHUNKS
W = BW + NA
OFFS = tuple(sum(CHUNKS[:i]) for i in range(len(CHUNKS)))
NK = len(CHUNKS)
assert NB + NA == FF
FIRST_LATE = 3
LATE = sum(CHUNKS[FIRST_LATE:])
EARLY = FF - LATE
N_REMOTE = 166
N_LOCAL = 48


SCHEDULE = (
    "Zu4", "Au0", "Zu1", "Ag0", "gz0", "Au4", "Au1", "Zg1", "gr0", "Zg0",
    "Xg1", "Bu4", "Zu0", "Ag1", "Zg3", "Qg0", "iz0", "Zg2", "dz0", "Bu1",
    "Ag3", "Qu0", "Bg1", "Xg0", "Fg0", "Bg0", "Bu0", "ir0", "Fg1", "Ag2",
    "Lg0", "Eg0", "dw0", "P3", "H0", "H1", "Lg1", "Xi0", "P4", "R3",
    "Zu2", "R4", "Eg1", "dw1", "P0", "S3", "P1", "Zg4", "Zu3", "D1",
    "R0", "R1", "Fi0", "S0", "D0", "P2", "S4", "G0", "R2", "Li0",
    "S1", "S2", "Au2", "Au3", "Ei0", "O0", "Bg3", "G1", "Bu3", "Bu2",
    "Bg2", "T2", "O1", "Ag4", "H2", "D2", "G2", "H3", "T4", "Bg4",
    "D3", "T3", "O2", "G4", "H4", "G3", "D4", "O4", "O3",
)


def is_b(k):
    return k < len(B_CHUNKS)


def is_s(k):
    return len(B_CHUNKS) <= k < len(B_CHUNKS) + len(S_CHUNKS)


def rs_width(k):
    return CHUNKS[k] // 2 if is_s(k) else CHUNKS[k]


def kernel(
    x_hbm, gate_hbm, up_hbm, go_hbm, down_hbm,
    og_hbm, ou_hbm, od_hbm, xt_hbm, late_g, late_u, late_h,
    grad, in_t, gate, up, gh, part, kept, far, near, swap_s, swap_r, dn_b, dn_a,
    hid_t, gg, gu, x_in, x_t, st_g, st_u, st_d,
    send_sem, recv_sem, local_sem,
):
    r = lax.axis_index("row")
    c = lax.axis_index("col")
    x, zh, core = r // 4, (r // 2) % 2, r % 2
    zl, y = c // 4, c % 4
    z = zh * 2 + zl

    def dev(x_, y_, z_, core_):
        return (x_ * 4 + (z_ // 2) * 2 + core_, (z_ % 2) * 4 + y_)

    zo = dev(x, y, (1 - zh) * 2 + 1 - zl, core)
    xp, xm = (dev((x + d) % 4, y, z, core) for d in (1, 3))
    yp, ym = (dev(x, (y + d) % 4, z, core) for d in (1, 3))
    sib = dev(x, y, z, 1 - core)
    mate = dev(x, y, zh * 2 + 1 - zl, core)
    y_prev, y_next, y_far = (y + 3) % 4, (y + 1) % 4, (y + 2) % 4

    barrier = pltpu.get_barrier_semaphore()
    peers = (mate, zo, xp, xm, yp, ym, sib)
    for peer in peers:
        pl.semaphore_signal(barrier, inc=1, device_id=peer, device_id_type=MESH)

    counts = {"remote": 0, "local": 0}
    started = []
    sent = set()

    def send(src, dst, to):
        i = counts["remote"]
        counts["remote"] += 1
        copy = pltpu.make_async_remote_copy(
            src_ref=src, dst_ref=dst, send_sem=send_sem.at[i], recv_sem=recv_sem.at[i],
            device_id=to, device_id_type=MESH,
        )
        copy.start()
        started.append(copy)
        return copy

    def local(src, dst):
        i = counts["local"]
        counts["local"] += 1
        copy = pltpu.make_async_copy(src, dst, local_sem.at[i])
        copy.start()
        return copy

    def al(v, n):
        return pl.multiple_of(v, n)

    def token_block(x_, zh_):
        return al(((x_ % 2) * 8 + zh_ * 4 + (x_ // 2) * 2 + core) * 128, 128)

    own_tok = token_block(x, zh)

    def rows_of(buf, tok, lanes):
        return buf.at[:, :, pl.ds(tok, 128)] if lanes else buf.at[:, pl.ds(tok, 128)]

    def one_of(buf, tok, lanes):
        return buf.at[zl, :, pl.ds(tok, 128)] if lanes else buf.at[zl, pl.ds(tok, 128)]

    def cols(k):
        return pl.ds(OFFS[k], CHUNKS[k])

    def rcols(k):
        return pl.ds(OFFS[k], rs_width(k))

    def dn_at(k):
        return OFFS[k] if is_b(k) else BW + (OFFS[k] - BW) // 2

    def swap_cols(k):
        return pl.ds(OFFS[k] - BW - NS, CHUNKS[k])

    def out_at(k, plane):
        if is_b(k):
            return pl.ds(al(plane * BW + OFFS[k], 128), CHUNKS[k])
        return pl.ds(OFFS[k] + BW, CHUNKS[k])

    def down_parts(plane):
        parts = [(pl.ds(al(plane * BW, 128), BW), pl.ds(0, BW))]
        for k in range(NK):
            if is_s(k):
                n = CHUNKS[k] // 2
                parts.append((
                    pl.ds(al(BW + OFFS[k] + plane * n, 128), n),
                    pl.ds(dn_at(k), n),
                ))
        return parts

    in_copy = local(x_hbm, x_in)
    own_grad = local(go_hbm, one_of(grad, own_tok, False))
    streams = {"g": (gate_hbm, gate), "u": (up_hbm, up)}
    own_chunk = {}
    z_chunk = {}
    ya_c, yb_c = {}, {}

    def load_chunk(s, k):
        hbm, buf = streams[s]
        own_chunk[s, k] = local(hbm.at[:, out_at(k, zl)], buf.at[y * 2 + zl, :, cols(k)])

    def z_send_chunk(s, k):
        hbm, buf = streams[s]
        z_chunk[s, k] = send(hbm.at[:, out_at(k, 1 - zl)], buf.at[y * 2 + zl, :, cols(k)], mate)

    for k in range(NK):
        for s in "gu":
            load_chunk(s, k)
    dn_copies = [
        local(down_hbm.at[src], dn_b.at[zl, dst]) for src, dst in down_parts(zl)
    ]
    dn_copy_a = local(down_hbm.at[pl.ds(NB + NS, NA - NS)], dn_a)

    pl.semaphore_wait(barrier, len(peers))

    def gather_a(buf, k):
        sl = buf.at[pl.ds(y * 2, 2), :, cols(k)]
        return send(sl, sl, yp), send(sl, sl, ym)

    def gather_b(buf, k, first):
        first[0].wait_recv()
        lo = buf.at[y_prev * 2, :, cols(k)]
        one = send(lo, lo, yp)
        first[1].wait_recv()
        hi = buf.at[y_next * 2 + 1, :, cols(k)]
        return one, send(hi, hi, ym)

    def ya(s, k):
        hbm, buf = streams[s]
        if k == 0:
            dst = buf.at[y * 2 + zl, :, cols(k)]
            src = hbm.at[:, out_at(k, zl)]
            ya_c[s, k] = send(src, dst, yp), send(src, dst, ym)
            return
        own_chunk[s, k].wait()
        z_chunk[s, k].wait_recv()
        ya_c[s, k] = gather_a(buf, k)

    def yq(s, k):
        buf = streams[s][1]
        own_chunk[s, k].wait()
        z_chunk[s, k].wait_recv()
        other = buf.at[y * 2 + 1 - zl, :, cols(k)]
        ya_c[s, k] += send(other, other, yp), send(other, other, ym)

    def yb(s, k):
        buf = streams[s][1]
        if k == 0:
            own_p, own_m, other_p, other_m = ya_c[s, k]
            own_p.wait_recv()
            lo = buf.at[y_prev * 2 + zl, :, cols(k)]
            one = send(lo, lo, yp)
            other_m.wait_recv()
            hi = buf.at[y_next * 2 + 1 - zl, :, cols(k)]
            yb_c[s, k] = one, send(hi, hi, ym), own_m, other_p
            return
        yb_c[s, k] = gather_b(buf, k, ya_c[s, k])

    def yc(s, k):
        for copy in yb_c[s, k]:
            copy.wait_recv()

    def row_z(src, buf, lanes):
        dst = one_of(buf, own_tok, lanes)
        return [send(src, dst, to) for to in (mate, zo)]

    def row_z_relay(buf, lanes, copies):
        copies[0].wait_recv()
        tok = pl.ds(own_tok, 128)
        ref = buf.at[1 - zl, :, tok] if lanes else buf.at[1 - zl, tok]
        copies.append(send(ref, ref, zo))

    def block(buf, x_, q, which, lanes):
        tok = pl.ds(token_block((x + x_) % 4, q), 128)
        if which == "both":
            return buf.at[:, :, tok] if lanes else buf.at[:, tok]
        half = zl if which == "own" else 1 - zl
        return buf.at[half, :, tok] if lanes else buf.at[half, tok]

    class Row:
        def __init__(self, buf, which, lanes):
            self.buf, self.which, self.lanes = buf, which, lanes
            self.core = []

        def move(self, x_, q, to):
            ref = block(self.buf, x_, q, self.which, self.lanes)
            return send(ref, ref, to)

        def to_core(self, x_):
            self.core += [self.move(x_, q, sib) for q in range(2)]

        def first(self, waits):
            for wait in waits:
                wait()
            self.up = [self.move(0, q, xp) for q in range(2)]
            self.down = [self.move(0, q, xm) for q in range(2)]
            self.to_core(0)

        def relay(self):
            self.up[0].wait_recv()
            self.far = [self.move(3, 0, xp)]
            self.down[1].wait_recv()
            self.far.append(self.move(1, 1, xm))
            self.up[1].wait_recv()
            self.to_core(3)
            self.down[0].wait_recv()
            self.to_core(1)

        def last(self):
            for copy in self.far:
                copy.wait_recv()
            self.to_core(2)

        def done(self):
            for copy in self.core:
                copy.wait_recv()

    def silu_parts(t, k):
        g = gate[t, :, cols(k)].astype(F32)
        u = up[t, :, cols(k)].astype(F32)
        s = jax.nn.sigmoid(g)
        return g, u, s

    keep = []

    def keep_late(buf, hbm, k):
        at = pl.ds(OFFS[k] - OFFS[FIRST_LATE], CHUNKS[k])
        keep.append(local(buf.at[:, :, cols(k)], hbm.at[:, :, at]))

    def make_hidden(k):
        yc("g", k)
        yc("u", k)
        if k >= FIRST_LATE:
            keep_late(gate, late_g, k)
            keep_late(up, late_u, k)

        def body(t, carry):
            g, u, s = silu_parts(t, k)
            h = (g * s * u).astype(BF)
            hid_t[cols(k), pl.ds(al(t * 256, 256), 256)] = h.T
            return carry

        lax.fori_loop(0, 8, body, 0)

    def nt(a, b):
        return lax.dot_general(a, b, (((1,), (1,)), ((), ())), preferred_element_type=F32)

    def partial_block(k, t):
        n = rs_width(k)
        rows = pl.ds(al(t * 256, 256), 256)
        if is_b(k) or is_s(k):
            acc = nt(grad[0, rows], dn_b[0, pl.ds(dn_at(k), n)])
            return acc + nt(grad[1, rows], dn_b[1, pl.ds(dn_at(k), n)])
        return nt(grad[zl, rows], dn_a[pl.ds(OFFS[k] - BW - NS, n)])

    def make_sent(k):
        def body(i, carry):
            d = 2 - (i // 2) * (1 - 2 * (i % 2))
            t = ((y + d) % 4) * 2 + (i // 2 + i) % 2
            part[t, :, rcols(k)] = partial_block(k, t).astype(BF)
            return carry

        lax.fori_loop(0, 4, body, 0)

    def make_kept(k):
        def body(i, carry):
            d = (i // 2) * (1 + 2 * (i % 2))
            t = ((y + d) % 4) * 2 + i % 2
            kept[i, :, rcols(k)] = partial_block(k, t)
            return carry

        lax.fori_loop(0, 4, body, 0)

    rs1, rs2, swaps, ha, hb = {}, {}, {}, {}, {}

    def rs_a(k):
        make_sent(k)
        cc = rcols(k)
        rs1[k] = (
            send(part.at[y_far * 2, :, cc], far.at[0, :, cc], yp),
            send(part.at[y_far * 2 + 1, :, cc], far.at[1, :, cc], ym),
            send(part.at[y_next * 2 + 1, :, cc], near.at[0, 1, :, cc], yp),
            send(part.at[y_prev * 2, :, cc], near.at[1, 0, :, cc], ym),
        )
        make_kept(k)

    def rs_b(k):
        cc = rcols(k)
        rs1[k][0].wait_recv()
        part[y_next * 2, :, cc] = (kept[2, :, cc] + far[0, :, cc].astype(F32)).astype(BF)
        one = send(part.at[y_next * 2, :, cc], near.at[0, 0, :, cc], yp)
        rs1[k][1].wait_recv()
        part[y_prev * 2 + 1, :, cc] = (kept[3, :, cc] + far[1, :, cc].astype(F32)).astype(BF)
        rs2[k] = (one, send(part.at[y_prev * 2 + 1, :, cc], near.at[1, 1, :, cc], ym))

    def rs_c(k):
        cc = rcols(k)
        n = rs_width(k)
        for copy in (rs1[k][2], rs1[k][3], rs2[k][0], rs2[k][1]):
            copy.wait_recv()
        if is_s(k):
            to = pl.ds(al(OFFS[k] + zl * n, 128), n)
        elif is_b(k):
            to = cols(k)
        for q in range(2):
            a = kept[q, :, cc] + near[0, q, :, cc].astype(F32) + near[1, q, :, cc].astype(F32)
            if is_b(k) or is_s(k):
                gh[y * 2 + q, :, to] = a.astype(BF)
            else:
                kept[q, :, cc] = a
                swap_s[q, :, swap_cols(k)] = a.astype(BF)
        if is_b(k):
            ha[k] = gather_a(gh, k)
        elif is_s(k):
            ref = gh.at[pl.ds(y * 2, 2), :, to]
            swaps[k] = send(ref, ref, mate)
        else:
            swaps[k] = send(swap_s.at[:, :, swap_cols(k)], swap_r.at[:, :, swap_cols(k)], mate)

    def rs_d(k):
        swaps[k].wait_recv()
        if not is_s(k):
            for q in range(2):
                a = kept[q, :, cols(k)] + swap_r[q, :, swap_cols(k)].astype(F32)
                gh[y * 2 + q, :, cols(k)] = a.astype(BF)
        ha[k] = gather_a(gh, k)

    def hg_b(k):
        hb[k] = gather_b(gh, k, ha[k])

    staged = {}

    def halves(k):
        return (zl, 1 - zl) if is_b(k) else (zl,)

    def clear(kind, k):
        for copy, is_remote in staged.pop((kind, k - 2), ()):
            if is_remote:
                copy.wait_send()
                sent.add(id(copy))
            else:
                copy.wait()

    def ship(kind, k, st, out, by_rows):
        n = CHUNKS[k]
        p = k % 2
        res = []
        for i in range(len(halves(k))):
            src = st.at[p, i, pl.ds(0, n), :] if by_rows else st.at[p, i, :, pl.ds(0, n)]
            dst = out.at[out_at(k, zl), :] if by_rows else out.at[:, out_at(k, zl)]
            res.append((local(src, dst), False) if i == 0 else (send(src, dst, mate), True))
        staged[kind, k] = res

    returned = []

    def down_grad(k):
        clear("d", k)
        n = CHUNKS[k]
        p = k % 2

        def body(m, carry):
            w = pl.ds(al(m * 512, 512), 512)
            for i, h in enumerate(halves(k)):
                acc = jnp.dot(hid_t[cols(k), :], grad[h, :, w], preferred_element_type=F32)
                st_d[p, i, pl.ds(0, n), w] = acc.astype(BF)
            return carry

        lax.fori_loop(0, 2, body, 0)
        ship("d", k, st_d, od_hbm, True)
        returned.extend(copy for copy, is_remote in staged["d", k] if is_remote)

    def weight_grads(k):
        for copy in hb[k]:
            copy.wait_recv()
        if k >= FIRST_LATE:
            keep_late(gh, late_h, k)
            return
        clear("g", k)
        clear("u", k)
        n = CHUNKS[k]
        p = k % 2

        def elem(t, carry):
            g, u, s = silu_parts(t, k)
            e = gh[t, :, cols(k)].astype(F32)
            rows = pl.ds(al(t * 256, 256), 256)
            gu[rows, pl.ds(0, n)] = (e * (g * s)).astype(BF)
            gg[rows, pl.ds(0, n)] = (e * u * s * (1.0 + g * (1.0 - s))).astype(BF)
            return carry

        lax.fori_loop(0, 8, elem, 0)

        def body(m, carry):
            w = pl.ds(al(m * 1024, 1024), 1024)
            for i, h in enumerate(halves(k)):
                lhs = in_t[h, w, :]
                acc = jnp.dot(lhs, gg[:, pl.ds(0, n)], preferred_element_type=F32)
                st_g[p, i, w, pl.ds(0, n)] = acc.astype(BF)
                acc = jnp.dot(lhs, gu[:, pl.ds(0, n)], preferred_element_type=F32)
                st_u[p, i, w, pl.ds(0, n)] = acc.astype(BF)
            return carry

        lax.fori_loop(0, 1, body, 0)
        for kind, st, out in (("g", st_g, og_hbm), ("u", st_u, ou_hbm)):
            ship(kind, k, st, out, False)
            returned.extend(copy for copy, is_remote in staged[kind, k] if is_remote)

    rows = {
        "g0": Row(grad, "own", False),
        "g1": Row(grad, "other", False),
        "i0": Row(in_t, "both", True),
    }
    zs = {}

    def grad_z(k):
        zs["g"] = row_z(go_hbm, grad, False)

    def in_z(k):
        in_copy.wait()
        x_t[...] = x_in[...].T
        zs["own"] = local(x_t, one_of(in_t, own_tok, True))
        zs["i"] = row_z(x_t, in_t, True)

    def row_first(s, k):
        if s == "i":
            waits = [zs["own"].wait] + [copy.wait_recv for copy in zs["i"][1:]]
        elif k == 0:
            waits = [own_grad.wait, zs["g"][2].wait_recv]
        else:
            waits = [zs["g"][1].wait_recv]
        rows[s + str(k)].first(waits)

    def row_done(s, k):
        rows[s + str(k)].done()
        if s == "i":
            keep.append(local(in_t.at[zl], xt_hbm))

    def down_z(k):
        zs["d"] = [send(down_hbm.at[src], dn_b.at[zl, dst], mate) for src, dst in down_parts(1 - zl)]

    def down_done(k):
        if k == 0:
            dn_copy_a.wait()
        else:
            for copy in dn_copies:
                copy.wait()
            for copy in zs["d"]:
                copy.wait_recv()

    events = {
        "Z": z_send_chunk, "A": ya, "Q": yq, "B": yb,
        "X": row_first,
        "F": lambda s, k: rows[s + str(k)].relay(),
        "L": lambda s, k: rows[s + str(k)].last(),
        "E": row_done,
        "gr": lambda k: row_z_relay(grad, False, zs["g"]),
        "ir": lambda k: row_z_relay(in_t, True, zs["i"]),
        "gz": grad_z, "iz": in_z, "dz": down_z, "dw": down_done,
        "H": make_hidden, "P": rs_a, "R": rs_b, "S": rs_c, "T": rs_d, "G": hg_b,
        "D": down_grad, "O": weight_grads,
    }
    for token in SCHEDULE:
        name, k = token[:-1], int(token[-1])
        if name in events:
            events[name](k)
        else:
            events[name[0]](name[1], k)

    for copies in staged.values():
        for copy, is_remote in copies:
            if not is_remote:
                copy.wait()
    for copy in keep:
        copy.wait()
    for copy in returned:
        copy.wait_recv()
    for copy in started:
        if id(copy) not in sent:
            copy.wait_send()
    assert counts["remote"] <= N_REMOTE and counts["local"] <= N_LOCAL


def late_kernel(
    og_in, ou_in, od_in, xt_hbm, g_hbm, u_hbm, h_hbm,
    og, ou, od,
    xt, gate, up, gh, gg, gu, st_g, st_u, buf_g, buf_u, buf_d, sems,
):
    counts = [0]

    def move(src, dst):
        copy = pltpu.make_async_copy(src, dst, sems.at[counts[0]])
        counts[0] += 1
        return copy

    def run(copies):
        for copy in copies:
            copy.start()

    first = [
        [move(src.at[pl.ds(i * 4, 4)], dst.at[pl.ds(i * 4, 4)]) for src, dst in
         ((h_hbm, gh), (g_hbm, gate), (u_hbm, up))]
        for i in range(2)
    ]
    second = [move(xt_hbm, xt)]
    n = 2
    loads, stores = {}, {}
    early = pl.ds(0, EARLY)
    for name, src, buf, dst in (
        ("d", od_in, buf_d, od), ("g", og_in, buf_g, og), ("u", ou_in, buf_u, ou),
    ):
        part = src.shape[0] // n
        loads[name], stores[name] = [], []
        for j in range(n):
            rows = pl.ds(j * part, part)
            at = (rows, slice(None)) if name == "d" else (rows, early)
            loads[name].append(move(src.at[at], buf.at[rows]))
            stores[name].append(move(buf.at[rows], dst.at[at]))
    run(first[0])
    run(first[1])
    run(second)
    for name in "dgu":
        run(loads[name])

    def elem(t, carry):
        g = gate[t].astype(F32)
        u = up[t].astype(F32)
        e = gh[t].astype(F32)
        s = jax.nn.sigmoid(g)
        rows = pl.ds(pl.multiple_of(t * 256, 256), 256)
        gu[rows] = (e * (g * s)).astype(BF)
        gg[rows] = (e * u * s * (1.0 + g * (1.0 - s))).astype(BF)
        return carry

    def pass_on(name):
        for load, store in zip(loads[name], stores[name]):
            load.wait()
            store.start()

    def matmul(dst, rhs):
        dst[...] = jnp.dot(xt[...], rhs[...], preferred_element_type=F32).astype(BF)

    for i in range(2):
        for copy in first[i]:
            copy.wait()
        lax.fori_loop(i * 4, i * 4 + 4, elem, 0)
    for copy in second:
        copy.wait()
    pass_on("d")
    matmul(st_g, gg)
    out_g = move(st_g, og.at[:, pl.ds(EARLY, LATE)])
    out_g.start()
    pass_on("g")
    pass_on("u")
    matmul(st_u, gu)
    out_u = move(st_u, ou.at[:, pl.ds(EARLY, LATE)])
    out_u.start()
    for name in "dgu":
        for store in stores[name]:
            store.wait()
    out_g.wait()
    out_u.wait()


def finish(og, ou, od, xt, g, u, h):
    any_spec = pl.BlockSpec(memory_space=pl.ANY)
    return pl.pallas_call(
        late_kernel,
        name="late_grads",
        out_shape=tuple(jax.ShapeDtypeStruct(a.shape, a.dtype) for a in (og, ou, od)),
        in_specs=[any_spec] * 7,
        out_specs=(any_spec,) * 3,
        scratch_shapes=[
            pltpu.VMEM((D, TOK), BF),
            pltpu.VMEM((8, 256, LATE), BF),
            pltpu.VMEM((8, 256, LATE), BF),
            pltpu.VMEM((8, 256, LATE), BF),
            pltpu.VMEM((TOK, LATE), BF),
            pltpu.VMEM((TOK, LATE), BF),
            pltpu.VMEM((D, LATE), BF),
            pltpu.VMEM((D, LATE), BF),
            pltpu.VMEM((D, EARLY), BF),
            pltpu.VMEM((D, EARLY), BF),
            pltpu.VMEM((FF, D), BF),
            pltpu.SemaphoreType.DMA((24,)),
        ],
        compiler_params=pltpu.CompilerParams(vmem_limit_bytes=62 * 2**20),
        cost_estimate=pl.CostEstimate(
            flops=4 * TOK * D * LATE, bytes_accessed=28 * 2**20, transcendentals=TOK * LATE
        ),
    )(og, ou, od, xt, g, u, h)


def on_device(inputs, gate_pre, up_pre, grad_out, down_weight):
    any_spec = pl.BlockSpec(memory_space=pl.ANY)
    return finish(*pl.pallas_call(
        kernel,
        name="swiglu_backward",
        out_shape=(
            jax.ShapeDtypeStruct((D, FF), BF),
            jax.ShapeDtypeStruct((D, FF), BF),
            jax.ShapeDtypeStruct((FF, D), BF),
            jax.ShapeDtypeStruct((D, TOK), BF),
            jax.ShapeDtypeStruct((8, 256, LATE), BF),
            jax.ShapeDtypeStruct((8, 256, LATE), BF),
            jax.ShapeDtypeStruct((8, 256, LATE), BF),
        ),
        in_specs=[any_spec] * 5,
        out_specs=(any_spec,) * 7,
        scratch_shapes=[
            pltpu.VMEM((2, TOK, D), BF),
            pltpu.VMEM((2, D, TOK), BF),
            pltpu.VMEM((8, 256, W), BF),
            pltpu.VMEM((8, 256, W), BF),
            pltpu.VMEM((8, 256, W), BF),
            pltpu.VMEM((8, 256, W), BF),
            pltpu.VMEM((4, 256, W), F32),
            pltpu.VMEM((2, 256, W), BF),
            pltpu.VMEM((2, 2, 256, W), BF),
            pltpu.VMEM((2, 256, NA - NS), BF),
            pltpu.VMEM((2, 256, NA - NS), BF),
            pltpu.VMEM((2, BW + NS // 2, D), BF),
            pltpu.VMEM((NA - NS, D), BF),
            pltpu.VMEM((W, TOK), BF),
            pltpu.VMEM((TOK, 256), BF),
            pltpu.VMEM((TOK, 256), BF),
            pltpu.VMEM((128, D), BF),
            pltpu.VMEM((D, 128), BF),
            pltpu.VMEM((2, 2, D, 256), BF),
            pltpu.VMEM((2, 2, D, 256), BF),
            pltpu.VMEM((2, 2, 256, D), BF),
            pltpu.SemaphoreType.DMA((N_REMOTE,)),
            pltpu.SemaphoreType.DMA((N_REMOTE,)),
            pltpu.SemaphoreType.DMA((N_LOCAL,)),
        ],
        compiler_params=pltpu.CompilerParams(
            collective_id=0, has_side_effects=True, vmem_limit_bytes=62 * 2**20
        ),
        cost_estimate=pl.CostEstimate(
            flops=8 * TOK * D * FF, bytes_accessed=40 * 2**20, transcendentals=TOK * FF
        ),
    )(inputs, gate_pre, up_pre, grad_out, down_weight))


def solution(mesh):
    placed = (P("row", "col"), P("col", "row"), P("col", "row"), P("row", "col"), P("row", "col"))
    return jax.shard_map(
        on_device,
        mesh=mesh,
        in_specs=placed,
        out_specs=(P("col", "row"), P("col", "row"), P("row", "col")),
        check_vma=False,
    )
```
